256 devices in a mesh: lat: 32 (over z, y_lo, core), lon: 8 (over y_hi, x).
Axes of the slice: x: 4, y: 4 (y_hi: 2, y_lo: 2; y = y_hi * 2 + y_lo), z: 8, core: 2. Of those that a mesh axis runs over, the one named last changes fastest.
Arguments:
- queries: bfloat16 [128, 256, 1024], P('lat', 'lon'), may hold values from -6 to 6
- keys: bfloat16 [128, 256, 1024], P('lat', 'lon'), may hold values from -6 to 6
- values: bfloat16 [128, 256, 1024], P('lat', 'lon'), may hold values from -6 to 6
- conv_kernel: float32 [9, 1024], replicated, may hold values from -2 to 2
- cotangent: bfloat16 [128, 256, 1024], P('lat', 'lon'), may hold values from -6 to 6
- pattern: int32 [128, 2], replicated, may hold values from -2 to 5, as said below
- polar: int32 [128], replicated, may hold values from 0 to 1, as said below
Outputs:
- mixed: bfloat16 [128, 256, 1024], P('lat', 'lon')
- query_grad: bfloat16 [128, 256, 1024], P('lat', 'lon')
- key_grad: bfloat16 [128, 256, 1024], P('lat', 'lon')
- value_grad: bfloat16 [128, 256, 1024], P('lat', 'lon')
- kernel_grad: float32 [9, 1024], replicated
The draws below stay inside these ranges and needn't reach their ends.
Inputs may be any that keep to these rules, and one draw needn't show every extreme that they name: `pattern`: column 0 of row i is o_i and column 1 is w_i, with -2 <= o_i <= 0 and 1 <= w_i <= 3 - o_i, so that the window of row i runs from o_i to o_i + w_i - 1 blocks around the query's block; some row spans 5 blocks. `polar`: 1 exactly on the first one to 2 and on the last one to 2 latitude rows, 0 on all others.
All inputs are finite; a program needn't handle non-finite values.
Results may differ from the reference program's by a relative error of at most 0.017.
Values may be sent and summed in bfloat16 or wider, within the bound.
No kernel may reach another device: no remote copies, remote signals or barrier semaphores. Data moves between devices by JAX's collectives and lax.ppermute only.
A program may use at most 128 MiB of HBM per device.

```python
import jax
import jax.numpy as jnp
from jax import lax

D = 1024
HEADS = 16
HEAD = 64
BLK = 8
REACH = 2
NLAT = 128
NLON = 256
NB = 32


def draw_queries(key, part):
    drawn = jnp.clip(jax.random.normal(jax.random.fold_in(key, 1), (NLAT, NLON, D), jnp.float32), -6.0, 6.0)
    return drawn.astype(jnp.bfloat16)


def draw_keys(key, part):
    drawn = jnp.clip(jax.random.normal(jax.random.fold_in(key, 2), (NLAT, NLON, D), jnp.float32), -6.0, 6.0)
    return drawn.astype(jnp.bfloat16)


def draw_pattern(key, part):
    left_reach = jax.random.randint(jax.random.fold_in(key, 21), (NLAT,), 0, REACH + 1)
    right_reach = jax.random.randint(jax.random.fold_in(key, 22), (NLAT,), 0, REACH + 1)
    chosen = jax.random.randint(jax.random.fold_in(key, 23), (), 0, NLAT)
    row_ids = jnp.arange(NLAT, dtype=jnp.int32)
    left_reach = jnp.where(row_ids == chosen, REACH, left_reach)
    right_reach = jnp.where(row_ids == chosen, REACH, right_reach)
    return jnp.stack((-left_reach, left_reach + right_reach + 1), axis=1).astype(jnp.int32)


def draw_polar(key, part):
    key = jax.random.fold_in(key, 31)
    counts = jax.random.randint(key, (5,), 0, REACH * REACH)
    combined = counts[2]
    north_rows = 1 + combined // REACH
    south_rows = 1 + combined % REACH
    row_ids = jnp.arange(NLAT, dtype=jnp.int32)
    return ((row_ids < north_rows) | (row_ids >= NLAT - south_rows)).astype(jnp.int32)


def block_scale(key, dims, shards, smallest, high):
    def one(axis_at, blocks):
        draws = jax.random.uniform(jax.random.fold_in(jax.random.fold_in(key, 6), axis_at), (blocks,), jnp.float32, smallest / len(shards), high / len(shards))
        return jnp.repeat(jnp.exp(draws), dims[axis_at] // blocks).reshape((-1,) + (1,) * (len(dims) - axis_at - 1))

    gain = one(*shards[0])
    for cut in shards[1:]:
        gain = gain * one(*cut)
    return gain


def normal_values(stream_key, dims, deviation, reach, shards=(), kind=jnp.bfloat16):
    values = deviation * jax.random.normal(stream_key, dims, jnp.float32)
    if shards:
        values = values * block_scale(stream_key, dims, shards, -0.22, 0.18)
    return jnp.clip(values, -reach, reach).astype(kind)


def setup_inputs(seed: int = 0) -> dict:
    key_of = jax.random.split(jax.random.key(seed), 8)
    queries = draw_queries(jax.random.fold_in(key_of[7], 71), 0)
    keys = draw_keys(jax.random.fold_in(key_of[7], 71), 0)
    values = normal_values(key_of[2], (NLAT, NLON, D), 1.0, 6.0, ((0, 32), (1, 8)))
    conv_kernel = normal_values(key_of[3], (9, D), 9 ** -0.5, 2.0, (), jnp.float32)
    cotangent = normal_values(key_of[4], (NLAT, NLON, D), 1.0, 6.0, ((0, 32), (1, 8)))
    pattern = draw_pattern(jax.random.fold_in(key_of[7], 71), 0)
    polar = draw_polar(jax.random.fold_in(key_of[7], 71), 0)
    return dict(queries=queries, keys=keys, values=values, conv_kernel=conv_kernel, cotangent=cotangent, pattern=pattern, polar=polar)


NEG = -1e+30

def widen(array):
    return array.astype(jnp.float32)

def block_window():
    blocks = jnp.arange(NB, dtype=jnp.int32)
    shifts = jnp.arange(2 * REACH + 1, dtype=jnp.int32) - REACH
    return (blocks[:, None] + shifts[None, :]) % NB

def window_take(rows_array, window):
    span = rows_array.shape[0]
    channels = rows_array.shape[-1]
    blocked = rows_array.reshape(span, NB, BLK, channels)
    taken = jnp.take(blocked, window, axis=1)
    taken = jnp.transpose(taken, (1, 0, 2, 3, 4))
    return taken.reshape(NB, span * window.shape[1] * BLK, channels)

def forward_row(row, queries, key_pad, value_pad, row_ok, offsets, widths, polar):
    window = block_window()
    span = 2 * REACH + 1
    score_scale = HEAD ** (-0.5)

    def near_rows():
        query_blocks = widen(queries[row]).reshape(NB, BLK, HEADS, HEAD)
        key_win = widen(window_take(lax.dynamic_slice_in_dim(key_pad, row, span, 0), window)).reshape(NB, -1, HEADS, HEAD)
        value_win = widen(window_take(lax.dynamic_slice_in_dim(value_pad, row, span, 0), window)).reshape(NB, -1, HEADS, HEAD)
        ok_rows = lax.dynamic_slice_in_dim(row_ok, row, span, 0)
        relative = jnp.arange(span, dtype=jnp.int32) - REACH - offsets[row]
        ok_blocks = (relative >= 0) & (relative < widths[row])
        allowed = jnp.broadcast_to(ok_rows[:, None, None] & ok_blocks[None, :, None], (span, span, BLK)).reshape(-1)
        scores = jnp.einsum('bqhd,bkhd->bhqk', query_blocks, key_win) * score_scale
        scores = jnp.where(allowed, scores, NEG)
        top = lax.optimization_barrier(jnp.max(scores, axis=-1))
        weights = jnp.where(allowed, jnp.exp(scores - top[..., None]), 0.0)
        total = lax.optimization_barrier(jnp.sum(weights, axis=-1))
        summed = jnp.einsum('bhqk,bkhd->bqhd', widen(weights.astype(jnp.bfloat16)), value_win)
        output = (summed / jnp.transpose(total, (0, 2, 1))[..., None]).reshape(NLON, D)
        lse = jnp.transpose(top + jnp.log(total), (0, 2, 1)).reshape(NLON, HEADS)
        return (output, lse)

    def whole_row():
        query_row = widen(queries[row]).reshape(NLON, HEADS, HEAD)
        key_row = widen(key_pad[row + REACH]).reshape(NLON, HEADS, HEAD)
        value_row = widen(value_pad[row + REACH]).reshape(NLON, HEADS, HEAD)
        scores = jnp.einsum('qhd,khd->hqk', query_row, key_row) * score_scale
        top = lax.optimization_barrier(jnp.max(scores, axis=-1))
        weights = jnp.exp(scores - top[..., None])
        total = lax.optimization_barrier(jnp.sum(weights, axis=-1))
        summed = jnp.einsum('hqk,khd->qhd', widen(weights.astype(jnp.bfloat16)), value_row)
        output = (summed / jnp.transpose(total)[..., None]).reshape(NLON, D)
        lse = jnp.transpose(top + jnp.log(total))
        return (output, lse)
    return lax.cond(polar[row] > 0, whole_row, near_rows)

def query_row_grad(row, queries, key_pad, value_pad, row_ok, offsets, widths, polar, d_att, lse, delta):
    window = block_window()
    span = 2 * REACH + 1
    score_scale = HEAD ** (-0.5)

    def near_rows():
        query_blocks = widen(queries[row]).reshape(NB, BLK, HEADS, HEAD)
        grad_blocks = widen(d_att[row]).reshape(NB, BLK, HEADS, HEAD)
        lse_blocks = jnp.transpose(lse[row].reshape(NB, BLK, HEADS), (0, 2, 1))
        delta_blocks = jnp.transpose(delta[row].reshape(NB, BLK, HEADS), (0, 2, 1))
        key_win = widen(window_take(lax.dynamic_slice_in_dim(key_pad, row, span, 0), window)).reshape(NB, -1, HEADS, HEAD)
        value_win = widen(window_take(lax.dynamic_slice_in_dim(value_pad, row, span, 0), window)).reshape(NB, -1, HEADS, HEAD)
        ok_rows = lax.dynamic_slice_in_dim(row_ok, row, span, 0)
        relative = jnp.arange(span, dtype=jnp.int32) - REACH - offsets[row]
        ok_blocks = (relative >= 0) & (relative < widths[row])
        allowed = jnp.broadcast_to(ok_rows[:, None, None] & ok_blocks[None, :, None], (span, span, BLK)).reshape(-1)
        scores = jnp.einsum('bqhd,bkhd->bhqk', query_blocks, key_win) * score_scale
        probs = jnp.where(allowed, jnp.exp(scores - lse_blocks[..., None]), 0.0)
        dprob = jnp.einsum('bqhd,bkhd->bhqk', grad_blocks, value_win)
        dscore = probs * (dprob - delta_blocks[..., None])
        grad = jnp.einsum('bhqk,bkhd->bqhd', widen(dscore.astype(jnp.bfloat16)), key_win) * score_scale
        return grad.reshape(NLON, D)

    def whole_row():
        query_row = widen(queries[row]).reshape(NLON, HEADS, HEAD)
        grad_row = widen(d_att[row]).reshape(NLON, HEADS, HEAD)
        key_row = widen(key_pad[row + REACH]).reshape(NLON, HEADS, HEAD)
        value_row = widen(value_pad[row + REACH]).reshape(NLON, HEADS, HEAD)
        scores = jnp.einsum('qhd,khd->hqk', query_row, key_row) * score_scale
        probs = jnp.exp(scores - jnp.transpose(lse[row])[..., None])
        dprob = jnp.einsum('qhd,khd->hqk', grad_row, value_row)
        dscore = probs * (dprob - jnp.transpose(delta[row])[..., None])
        grad = jnp.einsum('hqk,khd->qhd', widen(dscore.astype(jnp.bfloat16)), key_row) * score_scale
        return grad.reshape(NLON, D)
    return lax.cond(polar[row] > 0, whole_row, near_rows)

def key_row_grad(row, query_pad, grad_pad, lse_pad, delta_pad, ok_pad, offset_pad, width_pad, polar_pad, queries, keys, values, d_att, lse, delta, polar):
    window = block_window()
    span = 2 * REACH + 1
    score_scale = HEAD ** (-0.5)
    query_win = widen(window_take(lax.dynamic_slice_in_dim(query_pad, row, span, 0), window)).reshape(NB, -1, HEADS, HEAD)
    grad_win = widen(window_take(lax.dynamic_slice_in_dim(grad_pad, row, span, 0), window)).reshape(NB, -1, HEADS, HEAD)
    lse_win = jnp.transpose(window_take(lax.dynamic_slice_in_dim(lse_pad, row, span, 0), window), (0, 2, 1))
    delta_win = jnp.transpose(window_take(lax.dynamic_slice_in_dim(delta_pad, row, span, 0), window), (0, 2, 1))
    ok_query = lax.dynamic_slice_in_dim(ok_pad, row, span, 0) & (lax.dynamic_slice_in_dim(polar_pad, row, span, 0) == 0)
    offset_query = lax.dynamic_slice_in_dim(offset_pad, row, span, 0)
    width_query = lax.dynamic_slice_in_dim(width_pad, row, span, 0)
    relative = (REACH - jnp.arange(span, dtype=jnp.int32))[None, :] - offset_query[:, None]
    allowed = ok_query[:, None] & (relative >= 0) & (relative < width_query[:, None])
    allowed = jnp.broadcast_to(allowed[:, :, None], (span, span, BLK)).reshape(-1)
    key_blocks = widen(keys[row]).reshape(NB, BLK, HEADS, HEAD)
    value_blocks = widen(values[row]).reshape(NB, BLK, HEADS, HEAD)
    scores = jnp.einsum('bqhd,bkhd->bhqk', query_win, key_blocks) * score_scale
    probs = jnp.where(allowed[:, None], jnp.exp(scores - lse_win[..., None]), 0.0)
    dprob = jnp.einsum('bqhd,bkhd->bhqk', grad_win, value_blocks)
    dscore = probs * (dprob - delta_win[..., None])
    grad_key = jnp.einsum('bhqk,bqhd->bkhd', widen(dscore.astype(jnp.bfloat16)), query_win).reshape(NLON, D) * score_scale
    grad_value = jnp.einsum('bhqk,bqhd->bkhd', widen(probs.astype(jnp.bfloat16)), grad_win).reshape(NLON, D)

    def own_row():
        query_row = widen(queries[row]).reshape(NLON, HEADS, HEAD)
        grad_row = widen(d_att[row]).reshape(NLON, HEADS, HEAD)
        key_row = widen(keys[row]).reshape(NLON, HEADS, HEAD)
        value_row = widen(values[row]).reshape(NLON, HEADS, HEAD)
        row_scores = jnp.einsum('qhd,khd->hqk', query_row, key_row) * score_scale
        row_probs = jnp.exp(row_scores - jnp.transpose(lse[row])[..., None])
        row_dprob = jnp.einsum('qhd,khd->hqk', grad_row, value_row)
        row_dscore = row_probs * (row_dprob - jnp.transpose(delta[row])[..., None])
        extra_key = jnp.einsum('hqk,qhd->khd', widen(row_dscore.astype(jnp.bfloat16)), query_row) * score_scale
        extra_value = jnp.einsum('hqk,qhd->khd', widen(row_probs.astype(jnp.bfloat16)), grad_row)
        return (extra_key.reshape(NLON, D), extra_value.reshape(NLON, D))

    def no_row():
        return (jnp.zeros((NLON, D), jnp.float32), jnp.zeros((NLON, D), jnp.float32))
    extra_key, extra_value = lax.cond(polar[row] > 0, own_row, no_row)
    return (grad_key + extra_key, grad_value + extra_value)

def grid_pad(array):
    wrapped = jnp.concatenate([array[:, -1:], array, array[:, :1]], axis=1)
    return jnp.pad(wrapped, ((1, 1), (0, 0), (0, 0)))

def reference(queries, keys, values, conv_kernel, cotangent, pattern, polar):
    rim = ((REACH, REACH), (0, 0), (0, 0))
    key_pad = jnp.pad(keys, rim)
    value_pad = jnp.pad(values, rim)
    row_ok = jnp.pad(jnp.ones((NLAT,), jnp.int32), (REACH, REACH)) > 0
    offsets = pattern[:, 0]
    widths = pattern[:, 1]
    row_ids = jnp.arange(NLAT, dtype=jnp.int32)
    attended_wide, lse = lax.map(lambda row: forward_row(row, queries, key_pad, value_pad, row_ok, offsets, widths, polar), row_ids)
    attended = attended_wide.astype(jnp.bfloat16)
    att_pad = grid_pad(attended)
    cot_pad = grid_pad(cotangent)
    conv_sum = jnp.zeros((NLAT, NLON, D), jnp.float32)
    back = widen(cotangent)
    taps = []
    for tap_row in range(3):
        for tap_col in range(3):
            weight = conv_kernel[3 * tap_row + tap_col]
            shifted = widen(att_pad[tap_row:tap_row + NLAT, tap_col:tap_col + NLON])
            conv_sum = conv_sum + weight * shifted
            back = back + weight * widen(cot_pad[2 - tap_row:2 - tap_row + NLAT, 2 - tap_col:2 - tap_col + NLON])
            taps.append(lax.optimization_barrier(jnp.sum(widen(cotangent) * shifted, axis=(0, 1))))
    mixed = (widen(attended) + conv_sum).astype(jnp.bfloat16)
    d_att = back.astype(jnp.bfloat16)
    kernel_grad = jnp.stack(taps) * (NLAT * NLON) ** (-0.5)
    delta = jnp.einsum('ijhd,ijhd->ijh', widen(d_att).reshape(NLAT, NLON, HEADS, HEAD), widen(attended).reshape(NLAT, NLON, HEADS, HEAD))
    query_grad = lax.map(lambda row: query_row_grad(row, queries, key_pad, value_pad, row_ok, offsets, widths, polar, d_att, lse, delta), row_ids)
    query_pad = jnp.pad(queries, rim)
    grad_pad = jnp.pad(d_att, rim)
    lse_pad = jnp.pad(lse, rim)
    delta_pad = jnp.pad(delta, rim)
    offset_pad = jnp.pad(offsets, (REACH, REACH))
    width_pad = jnp.pad(widths, (REACH, REACH))
    polar_pad = jnp.pad(polar, (REACH, REACH))
    key_grad, value_grad = lax.map(lambda row: key_row_grad(row, query_pad, grad_pad, lse_pad, delta_pad, row_ok, offset_pad, width_pad, polar_pad, queries, keys, values, d_att, lse, delta, polar), row_ids)
    return (mixed, query_grad.astype(jnp.bfloat16), key_grad.astype(jnp.bfloat16), value_grad.astype(jnp.bfloat16), kernel_grad)
```

```python
import functools

import jax
import jax.numpy as jnp
import numpy as np
from jax import lax
from jax.experimental import pallas as pl
from jax.experimental.pallas import tpu as pltpu
from jax.sharding import PartitionSpec as P

HEADS = 16
HEAD = 64
BLK = 8
REACH = 2
NLAT = 128
NLON = 256
ROWS = 4
COLS = 32
SIDE = REACH * BLK
LANES = 128
PAIRS = 8
NEG = -1e30
SCALE = HEAD ** (-0.5)
F32 = jnp.float32
BF16 = jnp.bfloat16

LON_TOK = 144
LAT_TOK = 304
BACK_LAT = 288
BACK_LON = 144
POLE_IN = 320
POLE_OUT = 272


def params(mib, steps=1):
    return pltpu.CompilerParams(
        vmem_limit_bytes=mib * 2**20, dimension_semantics=("arbitrary",) * steps
    )


def lane_spec(*lead):
    zeros = (0,) * len(lead)
    return pl.BlockSpec(lead + (LANES,), lambda j: zeros + (j,))


SMEM = pl.BlockSpec(memory_space=pltpu.SMEM)


def nt(lhs, rhs):
    return lax.dot_general(lhs, rhs, (((1,), (1,)), ((), ())), preferred_element_type=F32)


def tn(lhs, rhs):
    return lax.dot_general(lhs, rhs, (((0,), (0,)), ((), ())), preferred_element_type=F32)


def nn(lhs, rhs):
    return lax.dot_general(lhs, rhs, (((1,), (0,)), ((), ())), preferred_element_type=F32)


def two_heads(array):
    first = lax.broadcasted_iota(jnp.int32, array.shape, 1) < HEAD
    return jnp.concatenate(
        [jnp.where(first, array, 0.0), jnp.where(first, 0.0, array)], axis=0
    ).astype(BF16)


def own_features(array):
    half = array.shape[1] // 2
    first = lax.broadcasted_iota(jnp.int32, (LANES, half), 0) < HEAD
    return jnp.where(first, array[:, :half], array[:, half:])


def attention(query, key, value, d_att, bias, valid):
    query2 = two_heads(query * SCALE)
    grad2 = two_heads(d_att)
    scores = nt(key, query2)
    if bias is not None:
        scores = scores + jnp.concatenate([bias, bias], axis=1)
    top = jnp.max(scores, axis=0, keepdims=True)
    weights = jnp.exp(scores - top)
    inverse = 1.0 / jnp.sum(weights, axis=0, keepdims=True)
    if valid is not None:
        inverse = inverse * jnp.concatenate([valid, valid], axis=1)
    att_t = own_features(tn(value, weights.astype(BF16)) * inverse).astype(BF16).astype(F32)
    product = d_att.T * att_t
    delta = jnp.concatenate(
        [
            jnp.sum(product[:HEAD], axis=0, keepdims=True),
            jnp.sum(product[HEAD:], axis=0, keepdims=True),
        ],
        axis=1,
    )
    probs = weights * inverse
    dscore = (probs * (nt(value, grad2) - delta)).astype(BF16)
    d_query = own_features(tn(key, dscore)).T * SCALE
    d_key = nn(dscore, query2)
    d_value = nn(probs.astype(BF16), grad2)
    return att_t.T, d_query, d_key, d_value


def pack_lon_kernel(pole_ref, q_ref, k_ref, v_ref, c_ref, east_ref, west_ref, pole_out, edge):
    half = ROWS * SIDE
    for out, start, col in ((east_ref, COLS - SIDE, COLS - 1), (west_ref, 0, 0)):
        out[0:half] = k_ref[:, start : start + SIDE].reshape(half, LANES)
        out[half : 2 * half] = v_ref[:, start : start + SIDE].reshape(half, LANES)
        edge[...] = jnp.zeros_like(edge)
        for row in range(ROWS):
            cells = c_ref[row].astype(F32)
            edge[row : row + 1] = cells[col : col + 1]
        out[2 * half :] = edge[...].astype(BF16)
    start = pole_ref[0]
    both = REACH * COLS
    pole_out[0, 0:both] = q_ref[pl.ds(start, REACH)].reshape(both, LANES)
    pole_out[0, both : 2 * both] = k_ref[pl.ds(start, REACH)].reshape(both, LANES)
    pole_out[0, 2 * both : 3 * both] = v_ref[pl.ds(start, REACH)].reshape(both, LANES)
    pole_out[0, 3 * both :] = c_ref[...].reshape(ROWS * COLS, LANES)


def pack_lat_kernel(k_ref, v_ref, c_ref, w_ref, e_ref, south_ref, north_ref, edge):
    own = REACH * COLS
    side = REACH * SIDE
    half = ROWS * SIDE
    west_cot = w_ref[2 * half :].astype(F32)
    east_cot = e_ref[2 * half :].astype(F32)
    for out, start, row in ((south_ref, ROWS - REACH, ROWS - 1), (north_ref, 0, 0)):
        for index, ref in enumerate((k_ref, v_ref)):
            base = index * (own + 2 * side)
            near = index * half + start * SIDE
            out[base : base + own] = ref[start : start + REACH].reshape(own, LANES)
            out[base + own : base + own + side] = w_ref[near : near + side]
            out[base + own + side : base + own + 2 * side] = e_ref[near : near + side]
        base = 2 * (own + 2 * side)
        out[base : base + COLS] = c_ref[row]
        edge[...] = jnp.zeros_like(edge)
        edge[0:1] = west_cot[row : row + 1]
        edge[1:2] = east_cot[row : row + 1]
        out[base + COLS :] = edge[...].astype(BF16)


def fill_rim(pad, row, middle, west, east):
    pad[row, 8 : 8 + COLS] = middle
    pad[row, 7:8] = west
    pad[row, 8 + COLS : 9 + COLS] = east


def window_kernel(
    q_ref, k_ref, v_ref, c_ref, w_ref, e_ref, n_ref, s_ref, conv_ref, bias_ref, valid_ref,
    att_ref, dq_ref, south_ref, north_ref, mid_ref, kg_ref, pad,
):
    tokens = ROWS * COLS
    half = ROWS * SIDE
    rim = 2 * REACH * SIDE + REACH * COLS
    west_cot = w_ref[2 * half :].astype(F32)
    east_cot = e_ref[2 * half :].astype(F32)
    for row in range(ROWS):
        fill_rim(
            pad, row + 1, c_ref[row].astype(F32), west_cot[row : row + 1], east_cot[row : row + 1]
        )
    for row, ref in ((0, n_ref), (ROWS + 1, s_ref)):
        cells = ref[2 * rim :].astype(F32)
        fill_rim(pad, row, cells[:COLS], cells[COLS : COLS + 1], cells[COLS + 1 : COLS + 2])
    back = c_ref[...].astype(F32)
    for a in range(3):
        for b in range(3):
            weight = conv_ref[3 * a + b : 3 * a + b + 1][None]
            back = back + weight * pad[2 - a : 2 - a + ROWS, 9 - b : 9 - b + COLS]
    d_att = back.astype(BF16).astype(F32).reshape(tokens, LANES)
    key = jnp.concatenate(
        [k_ref[...].reshape(tokens, LANES), w_ref[:half], e_ref[:half], n_ref[:rim], s_ref[:rim]],
        axis=0,
    )
    value = jnp.concatenate(
        [
            v_ref[...].reshape(tokens, LANES),
            w_ref[half : 2 * half],
            e_ref[half : 2 * half],
            n_ref[rim : 2 * rim],
            s_ref[rim : 2 * rim],
        ],
        axis=0,
    )
    query = q_ref[...].reshape(tokens, LANES).astype(F32)
    att, d_query, d_key, d_value = attention(
        query, key, value, d_att, bias_ref[...], valid_ref[...]
    )
    att_b = att.astype(BF16)
    att_ref[...] = att_b
    dq_ref[...] = d_query.astype(BF16)
    near = tokens + 2 * half
    mid_ref[0] = d_key[:near]
    mid_ref[1] = d_value[:near]
    for ref, start, row in ((north_ref, near, 0), (south_ref, near + rim, ROWS - 1)):
        ref[:rim] = d_key[start : start + rim].astype(BF16)
        ref[rim : 2 * rim] = d_value[start : start + rim].astype(BF16)
        ref[2 * rim :] = att_b[row * COLS : (row + 1) * COLS]
    att3 = att.reshape(ROWS, COLS, LANES)
    for a in range(3):
        for b in range(3):
            shifted = pad[2 - a : 2 - a + ROWS, 9 - b : 9 - b + COLS]
            total = jnp.sum((att3 * shifted).reshape(tokens, LANES), axis=0, keepdims=True)
            kg_ref[0, 3 * a + b : 3 * a + b + 1] = total


def pole_kernel(flag_ref, x_ref, conv_ref, y_ref, kg_ref, edge):
    both = REACH * COLS
    kg_ref[...] = jnp.zeros_like(kg_ref)

    @pl.when(flag_ref[1] + flag_ref[2] > 0)
    def _():
        edge[...] = jnp.zeros_like(edge)
        weights = conv_ref[0]
        rows = []
        for step in range(REACH + 2):
            row = flag_ref[0] + step - 1
            inside = jnp.where((row >= 0) & (row < ROWS), 1.0, 0.0)
            at = pl.multiple_of(3 * both + jnp.clip(row, 0, ROWS - 1) * COLS, COLS)
            rows.append(x_ref[:, pl.ds(at, COLS)].reshape(NLON, LANES).astype(F32) * inside)
        for r in range(REACH):
            taps = []
            back = rows[r + 1]
            for a in range(3):
                cells = rows[r + 2 - a]
                for b, shifted in enumerate(
                    (pltpu.roll(cells, NLON - 1, 0), cells, pltpu.roll(cells, 1, 0))
                ):
                    taps.append(shifted)
                    back = back + weights[3 * a + b : 3 * a + b + 1] * shifted
            query, key, value = (
                x_ref[:, part * both + r * COLS : part * both + (r + 1) * COLS].reshape(NLON, LANES)
                for part in range(3)
            )
            d_att = back.astype(BF16).astype(F32)
            att, d_query, d_key, d_value = attention(
                query.astype(F32), key, value, d_att, None, None
            )
            for part, array in enumerate((att, d_query, d_key, d_value)):
                y_ref[:, part * both + r * COLS : part * both + (r + 1) * COLS] = array.astype(
                    BF16
                ).reshape(PAIRS, COLS, LANES)
            for dest in range(PAIRS):
                west = (dest * COLS - 1) % NLON
                east = (dest * COLS + COLS) % NLON
                edge[dest, 2 * r : 2 * r + 1] = att[west : west + 1]
                edge[dest, 2 * r + 1 : 2 * r + 2] = att[east : east + 1]
            counted = jnp.where(flag_ref[1 + r] > 0, 1.0, 0.0)
            for tap in range(9):
                kg_ref[tap : tap + 1] += counted * jnp.sum(
                    att * taps[tap], axis=0, keepdims=True
                )
        y_ref[:, 4 * both :] = edge[...].astype(BF16)


def pack_back_kernel(mid_ref, att_ref, n_ref, s_ref, west_ref, east_ref, edge):
    half = ROWS * SIDE
    side = REACH * SIDE
    own = REACH * COLS
    rim = own + 2 * side
    for out, first, col in ((west_ref, 0, 0), (east_ref, 1, COLS - 1)):
        for index in range(2):
            source = index * rim + own + first * side
            cells = mid_ref[index, first * half : (first + 1) * half]
            out[index * half : index * half + side] = (
                cells[:side] + n_ref[source : source + side].astype(F32)
            ).astype(BF16)
            out[index * half + side : (index + 1) * half] = (
                cells[side:] + s_ref[source : source + side].astype(F32)
            ).astype(BF16)
        edge[...] = jnp.zeros_like(edge)
        edge[0:1] = n_ref[2 * rim :].astype(F32)[col : col + 1]
        edge[ROWS + 1 : ROWS + 2] = s_ref[2 * rim :].astype(F32)[col : col + 1]
        for row in range(ROWS):
            cells = att_ref[row * COLS : (row + 1) * COLS].astype(F32)
            edge[row + 1 : row + 2] = cells[col : col + 1]
        out[2 * half :] = edge[...].astype(BF16)


def final_kernel(
    flag_ref, att_ref, dq_ref, mid_ref, n_ref, s_ref, w_ref, e_ref, y_ref, conv_ref,
    mixed_out, dq_out, dk_out, dv_out, pad, dk_sum, dv_sum,
):
    half = ROWS * SIDE
    own = REACH * COLS
    both = own
    rim = own + 2 * REACH * SIDE
    west_att = w_ref[2 * half :].astype(F32)
    east_att = e_ref[2 * half :].astype(F32)
    middles = [n_ref[2 * rim :].astype(F32)]
    middles += [att_ref[row * COLS : (row + 1) * COLS].astype(F32) for row in range(ROWS)]
    middles += [s_ref[2 * rim :].astype(F32)]
    for row in range(ROWS + 2):
        fill_rim(pad, row, middles[row], west_att[row : row + 1], east_att[row : row + 1])
    dq_out[...] = dq_ref[...].reshape(ROWS, COLS, LANES)
    for index, total, factor in ((0, dk_sum, 1.0), (1, dv_sum, 1.0)):
        north = n_ref[index * rim : index * rim + own].astype(F32)
        south = s_ref[index * rim : index * rim + own].astype(F32)
        cells = mid_ref[index] + jnp.concatenate([north, south], axis=0)
        sides = jnp.concatenate(
            [
                w_ref[index * half : (index + 1) * half].astype(F32).reshape(ROWS, SIDE, LANES),
                e_ref[index * half : (index + 1) * half].astype(F32).reshape(ROWS, SIDE, LANES),
            ],
            axis=1,
        )
        total[...] = cells.reshape(ROWS, COLS, LANES) + sides
    start = flag_ref[0]
    for r in range(REACH):

        @pl.when(flag_ref[1 + r] > 0)
        def _():
            row = start + r
            ends = y_ref[0, 4 * both : POLE_OUT].astype(F32)
            part = [
                y_ref[0, p * both + r * COLS : p * both + (r + 1) * COLS] for p in range(4)
            ]
            fill_rim(
                pad,
                row + 1,
                part[0].astype(F32),
                ends[2 * r : 2 * r + 1],
                ends[2 * r + 1 : 2 * r + 2],
            )
            dq_out[row] = part[1]
            dk_sum[row] += part[2].astype(F32)
            dv_sum[row] += part[3].astype(F32)

    dk_out[...] = dk_sum[...].astype(BF16)
    dv_out[...] = dv_sum[...].astype(BF16)
    mixed = pad[1 : 1 + ROWS, 8 : 8 + COLS]
    for a in range(3):
        for b in range(3):
            weight = conv_ref[3 * a + b : 3 * a + b + 1][None]
            mixed = mixed + weight * pad[a : a + ROWS, 7 + b : 7 + b + COLS]
    mixed_out[...] = mixed.astype(BF16)


def key_places():
    rows, cols = [], []

    def add(row_range, col_range):
        for row in row_range:
            for col in col_range:
                rows.append(row)
                cols.append(col)

    inner, west, east = range(COLS), range(-SIDE, 0), range(COLS, COLS + SIDE)
    for part in (inner, west, east):
        add(range(ROWS), part)
    for row_range in (range(-REACH, 0), range(ROWS, ROWS + REACH)):
        for part in (inner, west, east):
            add(row_range, part)
    return np.array(rows, np.int32), np.array(cols, np.int32)


def shift(array, axis, step, wrap):
    count = lax.axis_size(axis)
    route = [(i, (i + step) % count) for i in range(count) if wrap or 0 <= i + step < count]
    return lax.ppermute(array, axis, route)


def sds(shape, dtype=BF16):
    return jax.ShapeDtypeStruct(shape, dtype)


def cost(flops, moved):
    return pl.CostEstimate(flops=flops, bytes_accessed=moved, transcendentals=0)


def body(queries, keys, values, conv_kernel, cotangent, pattern, polar):
    width = queries.shape[2]
    lat_count = lax.axis_size("lat")
    lat = lax.axis_index("lat")
    lon = lax.axis_index("lon")
    row_base = lat * ROWS
    tokens = ROWS * COLS
    full_rows = lane_spec(ROWS, COLS)
    edge = pltpu.VMEM((16, LANES), F32)
    rim_pad = pltpu.VMEM((ROWS + 2, 48, LANES), F32)

    own_polar = lax.dynamic_slice_in_dim(polar, row_base, ROWS, 0)
    pole_start = jnp.where(lat == 0, 0, ROWS - REACH).astype(jnp.int32)
    pole_flags = lax.dynamic_slice_in_dim(own_polar, pole_start, REACH, 0)
    flags = jnp.concatenate([pole_start[None], pole_flags]).astype(jnp.int32)

    east_pay, west_pay, pole_pay = pl.pallas_call(
        pack_lon_kernel,
        grid=(PAIRS,),
        in_specs=[SMEM] + [full_rows] * 4,
        out_specs=[
            lane_spec(LON_TOK),
            lane_spec(LON_TOK),
            pl.BlockSpec((1, POLE_IN, LANES), lambda j: (j, 0, 0)),
        ],
        out_shape=[
            sds((LON_TOK, width)),
            sds((LON_TOK, width)),
            sds((PAIRS, POLE_IN, LANES)),
        ],
        scratch_shapes=[edge],
        compiler_params=params(16),
        cost_estimate=cost(0, 3 * 2**20),
        name="pack_lon",
    )(flags, queries, keys, values, cotangent)
    from_west = shift(east_pay, "lon", 1, True)
    from_east = shift(west_pay, "lon", -1, True)
    pole_in = lax.all_to_all(pole_pay, "lon", 0, 0)

    south_pay, north_pay = pl.pallas_call(
        pack_lat_kernel,
        grid=(PAIRS,),
        in_specs=[full_rows] * 3 + [lane_spec(LON_TOK)] * 2,
        out_specs=[lane_spec(LAT_TOK)] * 2,
        out_shape=[sds((LAT_TOK, width))] * 2,
        scratch_shapes=[edge],
        compiler_params=params(16),
        cost_estimate=cost(0, 3 * 2**20),
        name="pack_lat",
    )(keys, values, cotangent, from_west, from_east)
    from_north = shift(south_pay, "lat", 1, False)
    from_south = shift(north_pay, "lat", -1, False)

    key_row, key_col = key_places()
    query_row, query_col = np.divmod(np.arange(tokens, dtype=np.int32), COLS)
    window = lax.dynamic_slice_in_dim(pattern, row_base, ROWS, 0)
    offset = jnp.repeat(window[:, 0], COLS)[None, :]
    count = jnp.repeat(window[:, 1], COLS)[None, :]
    distance = (key_col // BLK)[:, None] - (query_col // BLK)[None, :] - offset
    near = np.abs(key_row[:, None] - query_row[None, :]) <= REACH
    inside = (row_base + key_row >= 0) & (row_base + key_row < lat_count * ROWS)
    allowed = near & inside[:, None] & (distance >= 0) & (distance < count)
    bias = jnp.where(allowed, 0.0, NEG).astype(F32)
    valid = jnp.repeat(jnp.where(own_polar > 0, 0.0, 1.0).astype(F32), COLS)[None, :]

    pole_out, pole_kg = pl.pallas_call(
        pole_kernel,
        in_specs=[
            SMEM,
            pl.BlockSpec(memory_space=pltpu.VMEM),
            pl.BlockSpec(memory_space=pltpu.VMEM),
        ],
        out_specs=[pl.BlockSpec(memory_space=pltpu.VMEM)] * 2,
        out_shape=[sds((PAIRS, POLE_OUT, LANES)), sds((16, LANES), F32)],
        scratch_shapes=[pltpu.VMEM((PAIRS, 16, LANES), F32)],
        compiler_params=params(24, 0),
        cost_estimate=cost(10**9, 4 * 2**20),
        name="pole",
    )(
        flags,
        pole_in,
        lax.dynamic_slice_in_dim(
            conv_kernel.reshape(9, PAIRS, LANES), lon, 1, 1
        ).reshape(1, 9, LANES),
    )

    att, dq_near, south_back, north_back, mid, kg = pl.pallas_call(
        window_kernel,
        grid=(PAIRS,),
        in_specs=[full_rows] * 4
        + [lane_spec(LON_TOK)] * 2
        + [lane_spec(LAT_TOK)] * 2
        + [
            lane_spec(9),
            pl.BlockSpec((4 * tokens, tokens), lambda j: (0, 0)),
            pl.BlockSpec((1, tokens), lambda j: (0, 0)),
        ],
        out_specs=[
            lane_spec(tokens),
            lane_spec(tokens),
            lane_spec(BACK_LAT),
            lane_spec(BACK_LAT),
            lane_spec(2, 2 * tokens),
            pl.BlockSpec((1, 16, LANES), lambda j: (j, 0, 0)),
        ],
        out_shape=[
            sds((tokens, width)),
            sds((tokens, width)),
            sds((BACK_LAT, width)),
            sds((BACK_LAT, width)),
            sds((2, 2 * tokens, width), F32),
            sds((PAIRS, 16, LANES), F32),
        ],
        scratch_shapes=[rim_pad],
        compiler_params=params(24),
        cost_estimate=cost(4 * 10**9, 8 * 2**20),
        name="window",
    )(
        queries, keys, values, cotangent, from_west, from_east, from_north, from_south,
        conv_kernel, bias, valid,
    )

    back_north = shift(south_back, "lat", 1, False)
    back_south = shift(north_back, "lat", -1, False)

    mine = (jnp.arange(PAIRS) == lon)[:, None, None]
    kg = (kg + jnp.where(mine, pole_kg[None], 0.0))[:, :9].reshape(PAIRS * 9, LANES)
    high = lax.reduce_precision(kg, 8, 7)
    low = kg - high
    kg_pay = jnp.concatenate([high, low], axis=0).astype(BF16)
    back_pay = jnp.concatenate(
        [pole_out, jnp.broadcast_to(kg_pay[None], (PAIRS,) + kg_pay.shape)], axis=1
    )
    pole_back = lax.all_to_all(back_pay, "lon", 0, 0)
    kg_parts = jnp.sum(pole_back[:, POLE_OUT:].astype(F32), axis=0)
    kg_sum = kg_parts[: PAIRS * 9] + kg_parts[PAIRS * 9 :]
    step = 1
    while step < lat_count:
        kg_sum = kg_sum + lax.ppermute(kg_sum, "lat", [(i, i ^ step) for i in range(lat_count)])
        step *= 2
    norm_factor = (NLAT * NLON) ** (-0.5)
    kernel_grad = (
        jnp.transpose(kg_sum.reshape(PAIRS, 9, LANES), (1, 0, 2)).reshape(9, width) * norm_factor
    )

    west_back, east_back = pl.pallas_call(
        pack_back_kernel,
        grid=(PAIRS,),
        in_specs=[
            pl.BlockSpec((2, tokens, LANES), lambda j: (0, 1, j)),
            lane_spec(tokens),
            lane_spec(BACK_LAT),
            lane_spec(BACK_LAT),
        ],
        out_specs=[lane_spec(BACK_LON)] * 2,
        out_shape=[sds((BACK_LON, width))] * 2,
        scratch_shapes=[edge],
        compiler_params=params(16),
        cost_estimate=cost(0, 3 * 2**20),
        name="pack_back",
    )(mid, att, back_north, back_south)
    back_east = shift(west_back, "lon", -1, True)
    back_west = shift(east_back, "lon", 1, True)

    total_tok = POLE_OUT + 18 * PAIRS
    mixed, query_grad, key_grad, value_grad = pl.pallas_call(
        final_kernel,
        grid=(PAIRS,),
        in_specs=[
            SMEM,
            lane_spec(tokens),
            lane_spec(tokens),
            pl.BlockSpec((2, tokens, LANES), lambda j: (0, 0, j)),
            lane_spec(BACK_LAT),
            lane_spec(BACK_LAT),
            lane_spec(BACK_LON),
            lane_spec(BACK_LON),
            pl.BlockSpec((1, total_tok, LANES), lambda j: (j, 0, 0)),
            lane_spec(9),
        ],
        out_specs=[full_rows] * 4,
        out_shape=[sds((ROWS, COLS, width))] * 4,
        scratch_shapes=[rim_pad, pltpu.VMEM((ROWS, COLS, LANES), F32), pltpu.VMEM((ROWS, COLS, LANES), F32)],
        compiler_params=params(24),
        cost_estimate=cost(0, 6 * 2**20),
        name="final",
    )(
        flags, att, dq_near, mid, back_north, back_south, back_west, back_east, pole_back,
        conv_kernel,
    )
    return mixed, query_grad, key_grad, value_grad, kernel_grad


def solution(mesh):
    return jax.shard_map(
        body,
        mesh=mesh,
        in_specs=(
            P("lat", "lon", None),
            P("lat", "lon", None),
            P("lat", "lon", None),
            P(),
            P("lat", "lon", None),
            P(),
            P(),
        ),
        out_specs=(
            P("lat", "lon", None),
            P("lat", "lon", None),
            P("lat", "lon", None),
            P("lat", "lon", None),
            P(),
        ),
        check_vma=False,
    )
```

```python
import functools

import jax
import jax.numpy as jnp
from jax import lax
from jax.experimental import pallas as pl
from jax.experimental.pallas import tpu as pltpu
from jax.sharding import PartitionSpec as P

HEADS = 16
HEAD = 64
BLK = 8
REACH = 2
NLAT = 128
NLON = 256
ROWS = 4
COLS = 32
SIDE = REACH * BLK
LANES = 128
PAIRS = 8
NEG = -1e30
SCALE = HEAD ** (-0.5)
F32 = jnp.float32
BF16 = jnp.bfloat16
GRANT = 64

LON_TOK = 144
LAT_TOK = 304
BACK_LAT = 288
BACK_LON = 144
POLE_IN = 320
KG_ROWS = 80
POLE_OUT = 272


def params(mib, steps=1):
    return pltpu.CompilerParams(
        vmem_limit_bytes=mib * 2**20, dimension_semantics=("arbitrary",) * steps
    )


def lane_spec(*lead, wide=LANES):
    zeros = (0,) * len(lead)
    return pl.BlockSpec(lead + (wide,), lambda j: zeros + (j,))


SMEM = pl.BlockSpec(memory_space=pltpu.SMEM)


def nt(lhs, rhs):
    return lax.dot_general(lhs, rhs, (((1,), (1,)), ((), ())), preferred_element_type=F32)


def tn(lhs, rhs):
    return lax.dot_general(lhs, rhs, (((0,), (0,)), ((), ())), preferred_element_type=F32)


def nn(lhs, rhs):
    return lax.dot_general(lhs, rhs, (((1,), (0,)), ((), ())), preferred_element_type=F32)


def two_heads(array):
    first = lax.broadcasted_iota(jnp.int32, array.shape, 1) < HEAD
    return jnp.concatenate(
        [jnp.where(first, array, 0.0), jnp.where(first, 0.0, array)], axis=0
    ).astype(BF16)


def own_features(array):
    half = array.shape[1] // 2
    first = lax.broadcasted_iota(jnp.int32, (LANES, half), 0) < HEAD
    return jnp.where(first, array[:, :half], array[:, half:])


def attention(query, key, value, d_att, bias, valid):
    query2 = two_heads(query * SCALE)
    grad2 = two_heads(d_att)
    scores = nt(key, query2)
    if bias is not None:
        scores = scores + jnp.concatenate([bias, bias], axis=1)
    top = jnp.max(scores, axis=0, keepdims=True)
    weights = jnp.exp(scores - top)
    inverse = 1.0 / jnp.sum(weights, axis=0, keepdims=True)
    if valid is not None:
        inverse = inverse * jnp.concatenate([valid, valid], axis=1)
    att_t = own_features(tn(value, weights.astype(BF16)) * inverse).astype(BF16).astype(F32)
    product = d_att.T * att_t
    delta = jnp.concatenate(
        [
            jnp.sum(product[:HEAD], axis=0, keepdims=True),
            jnp.sum(product[HEAD:], axis=0, keepdims=True),
        ],
        axis=1,
    )
    probs = weights * inverse
    dscore = (probs * (nt(value, grad2) - delta)).astype(BF16)
    d_query = own_features(tn(key, dscore)).T * SCALE
    d_key = nn(dscore, query2)
    d_value = nn(probs.astype(BF16), grad2)
    return att_t.T, d_query, d_key, d_value


def place():
    lat = lax.axis_index("lat")
    return lat, lax.axis_index("lon"), jnp.where(lat == 0, 0, ROWS - REACH)


def at_pole(lat):
    return (lat == 0) | (lat == NLAT // ROWS - 1)


def run_copies(pairs, sems):
    copies = [
        pltpu.make_async_copy(source, target, sems.at[index])
        for index, (source, target) in enumerate(pairs)
    ]
    for copy in copies:
        copy.start()
    for copy in copies:
        copy.wait()


def pack_lon_kernel(q_ref, k_ref, v_ref, c_ref, east_ref, west_ref, pole_out, edge):
    half = ROWS * SIDE
    wide = edge.shape[1]
    for out, start, col in ((east_ref, COLS - SIDE, COLS - 1), (west_ref, 0, 0)):
        out[0:half] = k_ref[:, start : start + SIDE].reshape(half, wide)
        out[half : 2 * half] = v_ref[:, start : start + SIDE].reshape(half, wide)
        edge[...] = jnp.zeros_like(edge)
        for row in range(ROWS):
            cells = c_ref[row].astype(F32)
            edge[row : row + 1] = cells[col : col + 1]
        out[2 * half :] = edge[...].astype(BF16)
    lat, lon, start = place()
    both = REACH * COLS

    @pl.when(at_pole(lat))
    def _():
        for part in range(wide // LANES):
            lanes = slice(part * LANES, (part + 1) * LANES)
            for index, ref in enumerate((q_ref, k_ref, v_ref)):
                pole_out[part, index * both : (index + 1) * both] = ref[
                    pl.ds(start, REACH), :, lanes
                ].reshape(both, LANES)
            pole_out[part, 3 * both :] = c_ref[:, :, lanes].reshape(ROWS * COLS, LANES)


def pack_lat_kernel(k_ref, v_ref, c_ref, w_ref, e_ref, south_ref, north_ref, edge):
    own = REACH * COLS
    side = REACH * SIDE
    half = ROWS * SIDE
    wide = edge.shape[1]
    west_cot = w_ref[2 * half :].astype(F32)
    east_cot = e_ref[2 * half :].astype(F32)
    for out, start, row in ((south_ref, ROWS - REACH, ROWS - 1), (north_ref, 0, 0)):
        for index, ref in enumerate((k_ref, v_ref)):
            base = index * (own + 2 * side)
            near = index * half + start * SIDE
            out[base : base + own] = ref[start : start + REACH].reshape(own, wide)
            out[base + own : base + own + side] = w_ref[near : near + side]
            out[base + own + side : base + own + 2 * side] = e_ref[near : near + side]
        base = 2 * (own + 2 * side)
        out[base : base + COLS] = c_ref[row]
        edge[...] = jnp.zeros_like(edge)
        edge[0:1] = west_cot[row : row + 1]
        edge[1:2] = east_cot[row : row + 1]
        out[base + COLS :] = edge[...].astype(BF16)


def fill_rim(pad, row, middle, west, east):
    pad[row, 8 : 8 + COLS] = middle
    pad[row, 7:8] = west
    pad[row, 8 + COLS : 9 + COLS] = east


def key_groups():
    groups, start = [], 0
    for row_range in ((0, ROWS), (-REACH, REACH), (ROWS, REACH)):
        for first_col, width in ((0, COLS), (-SIDE, SIDE), (COLS, SIDE)):
            size = row_range[1] * width
            groups.append((start, size, row_range[0], width, first_col))
            start += size
    return groups


def window_kernel(
    pattern_ref, polar_ref, q_ref, k_ref, v_ref, c_ref, w_ref, e_ref, n_ref, s_ref, conv_ref,
    att_ref, dq_ref, south_ref, north_ref, mid_ref, kg_ref, pad, bias_ref,
):
    tokens = ROWS * COLS
    base = lax.axis_index("lat") * ROWS
    query_at = lax.broadcasted_iota(jnp.int32, (1, tokens), 1)
    query_row = query_at >> COLS.bit_length() - 1

    def by_row(values):
        out = jnp.full((1, tokens), values[0], values[0].dtype)
        for row in range(1, ROWS):
            out = jnp.where(query_row == row, values[row], out)
        return out

    valid = by_row([jnp.where(polar_ref[base + row] > 0, 0.0, 1.0) for row in range(ROWS)])

    @pl.when(pl.program_id(0) == 0)
    def _():
        offset = by_row([pattern_ref[0, base + row] for row in range(ROWS)])
        count = by_row([pattern_ref[1, base + row] for row in range(ROWS)])
        bits = BLK.bit_length() - 1
        block = ((query_at & COLS - 1) >> bits) + offset
        for start, size, first_row, width, first_col in key_groups():
            index = lax.broadcasted_iota(jnp.int32, (size, tokens), 0)
            row = (index >> width.bit_length() - 1) + first_row
            distance = ((index & width - 1) >> bits) + first_col // BLK - block
            inside = (jnp.abs(row - query_row) <= REACH) & (distance >= 0) & (distance < count)
            inside = inside & (base + row >= 0) & (base + row < NLAT)
            bias_ref[start : start + size] = jnp.where(inside, 0.0, NEG)

    half = ROWS * SIDE
    rim = 2 * REACH * SIDE + REACH * COLS
    wide = pad.shape[2]
    west_cot = w_ref[2 * half :].astype(F32)
    east_cot = e_ref[2 * half :].astype(F32)
    for row in range(ROWS):
        fill_rim(
            pad, row + 1, c_ref[row].astype(F32), west_cot[row : row + 1], east_cot[row : row + 1]
        )
    for row, ref in ((0, n_ref), (ROWS + 1, s_ref)):
        cells = ref[2 * rim :].astype(F32)
        fill_rim(pad, row, cells[:COLS], cells[COLS : COLS + 1], cells[COLS + 1 : COLS + 2])
    for part in range(wide // LANES):
        lanes = slice(part * LANES, (part + 1) * LANES)
        taps = [
            pad[2 - a : 2 - a + ROWS, 9 - b : 9 - b + COLS, lanes].reshape(tokens, LANES)
            for a in range(3)
            for b in range(3)
        ]
        back = taps[4]
        for tap in range(9):
            back = back + conv_ref[tap : tap + 1, lanes] * taps[tap]
        d_att = back.astype(BF16).astype(F32)
        key, value = (
            jnp.concatenate(
                [
                    ref[:, :, lanes].reshape(tokens, LANES),
                    w_ref[index * half : (index + 1) * half, lanes],
                    e_ref[index * half : (index + 1) * half, lanes],
                    n_ref[index * rim : (index + 1) * rim, lanes],
                    s_ref[index * rim : (index + 1) * rim, lanes],
                ],
                axis=0,
            )
            for index, ref in enumerate((k_ref, v_ref))
        )
        query = q_ref[:, :, lanes].reshape(tokens, LANES).astype(F32)
        att, d_query, d_key, d_value = attention(
            query, key, value, d_att, bias_ref[...], valid
        )
        att_b = att.astype(BF16)
        att_ref[:, lanes] = att_b
        dq_ref[:, lanes] = d_query.astype(BF16)
        near = tokens + 2 * half
        mid_ref[0, :, lanes] = d_key[:near]
        mid_ref[1, :, lanes] = d_value[:near]
        for ref, start, row in ((north_ref, near, 0), (south_ref, near + rim, ROWS - 1)):
            ref[:rim, lanes] = d_key[start : start + rim].astype(BF16)
            ref[rim : 2 * rim, lanes] = d_value[start : start + rim].astype(BF16)
            ref[2 * rim :, lanes] = att_b[row * COLS : (row + 1) * COLS]
        for tap in range(9):
            kg_ref[tap : tap + 1, lanes] = jnp.sum(att * taps[tap], axis=0, keepdims=True)


def pole_kernel(
    polar_ref, pole_in_ref, conv_ref, kgin_ref,
    out_ref, x_ref, y_ref, edge, weights_ref, kg_ref, kg_rows, kg_pair, sems,
):
    both = REACH * COLS
    lat, lon, start = place()
    base = lat * ROWS + start
    mine = pl.ds(pl.multiple_of(lon * LANES, LANES), LANES)
    run_copies([(kgin_ref, kg_ref)], sems)

    @pl.when(at_pole(lat))
    def _():
        run_copies([(conv_ref.at[:, mine], weights_ref), (pole_in_ref, x_ref)], sems)
        edge[...] = jnp.zeros_like(edge)
        weights = weights_ref[...]
        rows = []
        for step in range(REACH + 2):
            row = start + step - 1
            inside = jnp.where((row >= 0) & (row < ROWS), 1.0, 0.0)
            at = pl.multiple_of(3 * both + jnp.clip(row, 0, ROWS - 1) * COLS, COLS)
            rows.append(x_ref[:, pl.ds(at, COLS)].reshape(NLON, LANES).astype(F32) * inside)
        for r in range(REACH):
            taps = []
            back = rows[r + 1]
            for a in range(3):
                cells = rows[r + 2 - a]
                for b, shifted in enumerate(
                    (pltpu.roll(cells, NLON - 1, 0), cells, pltpu.roll(cells, 1, 0))
                ):
                    taps.append(shifted)
                    back = back + weights[3 * a + b : 3 * a + b + 1] * shifted
            query, key, value = (
                x_ref[:, part * both + r * COLS : part * both + (r + 1) * COLS].reshape(NLON, LANES)
                for part in range(3)
            )
            d_att = back.astype(BF16).astype(F32)
            att, d_query, d_key, d_value = attention(
                query.astype(F32), key, value, d_att, None, None
            )
            for part, array in enumerate((att, d_query, d_key, d_value)):
                y_ref[:, part * both + r * COLS : part * both + (r + 1) * COLS] = array.astype(
                    BF16
                ).reshape(PAIRS, COLS, LANES)
            for dest in range(PAIRS):
                west = (dest * COLS - 1) % NLON
                east = (dest * COLS + COLS) % NLON
                edge[dest, 2 * r : 2 * r + 1] = att[west : west + 1]
                edge[dest, 2 * r + 1 : 2 * r + 2] = att[east : east + 1]
            counted = jnp.where(polar_ref[base + r] > 0, 1.0, 0.0)
            for tap in range(9):
                kg_ref[tap : tap + 1, mine] += counted * jnp.sum(
                    att * taps[tap], axis=0, keepdims=True
                )
        y_ref[:, 4 * both :] = edge[...].astype(BF16)
        run_copies([(y_ref, out_ref.at[:, pl.ds(0, POLE_OUT)])], sems)

    kg_rows[...] = jnp.zeros_like(kg_rows)
    for block in range(PAIRS):
        kg_rows[9 * block : 9 * (block + 1)] = kg_ref[:, block * LANES : (block + 1) * LANES]
    high = kg_rows[...].astype(BF16)
    kg_pair[:KG_ROWS] = high
    kg_pair[KG_ROWS:] = (kg_rows[...] - high.astype(F32)).astype(BF16)
    tail = pl.ds(POLE_OUT, 2 * KG_ROWS)
    run_copies([(kg_pair, out_ref.at[dest, tail]) for dest in range(PAIRS)], sems)


def pack_back_kernel(mid_ref, att_ref, n_ref, s_ref, west_ref, east_ref, edge):
    half = ROWS * SIDE
    side = REACH * SIDE
    own = REACH * COLS
    rim = own + 2 * side
    for out, first, col in ((west_ref, 0, 0), (east_ref, 1, COLS - 1)):
        for index in range(2):
            source = index * rim + own + first * side
            cells = mid_ref[index, first * half : (first + 1) * half]
            out[index * half : index * half + side] = (
                cells[:side] + n_ref[source : source + side].astype(F32)
            ).astype(BF16)
            out[index * half + side : (index + 1) * half] = (
                cells[side:] + s_ref[source : source + side].astype(F32)
            ).astype(BF16)
        edge[...] = jnp.zeros_like(edge)
        edge[0:1] = n_ref[2 * rim :].astype(F32)[col : col + 1]
        edge[ROWS + 1 : ROWS + 2] = s_ref[2 * rim :].astype(F32)[col : col + 1]
        for row in range(ROWS):
            cells = att_ref[row * COLS : (row + 1) * COLS].astype(F32)
            edge[row + 1 : row + 2] = cells[col : col + 1]
        out[2 * half :] = edge[...].astype(BF16)


def final_kernel(
    polar_ref, att_ref, dq_ref, mid_ref, n_ref, s_ref, w_ref, e_ref,
    back_ref, conv_ref,
    mixed_out, dq_out, dk_out, dv_out, pad, dk_sum, dv_sum, y_ref, sems,
):
    half = ROWS * SIDE
    own = REACH * COLS
    both = own
    rim = own + 2 * REACH * SIDE
    west_att = w_ref[2 * half :].astype(F32)
    east_att = e_ref[2 * half :].astype(F32)
    middles = [n_ref[2 * rim :].astype(F32)]
    middles += [att_ref[row * COLS : (row + 1) * COLS].astype(F32) for row in range(ROWS)]
    middles += [s_ref[2 * rim :].astype(F32)]
    for row in range(ROWS + 2):
        fill_rim(pad, row, middles[row], west_att[row : row + 1], east_att[row : row + 1])
    dq_out[...] = dq_ref[...].reshape(ROWS, COLS, -1)
    wide = pad.shape[2]
    for index, total in ((0, dk_sum), (1, dv_sum)):
        north = n_ref[index * rim : index * rim + own].astype(F32)
        south = s_ref[index * rim : index * rim + own].astype(F32)
        cells = mid_ref[index] + jnp.concatenate([north, south], axis=0)
        sides = jnp.concatenate(
            [
                w_ref[index * half : (index + 1) * half].astype(F32).reshape(ROWS, SIDE, wide),
                e_ref[index * half : (index + 1) * half].astype(F32).reshape(ROWS, SIDE, wide),
            ],
            axis=1,
        )
        total[...] = cells.reshape(ROWS, COLS, wide) + sides
    lat, lon, start = place()

    @pl.when(at_pole(lat) & (pl.program_id(0) == 0))
    def _():
        run_copies([(back_ref.at[:, pl.ds(0, POLE_OUT)], y_ref)], sems)

    for r in range(REACH):

        @pl.when(at_pole(lat) & (polar_ref[lat * ROWS + start + r] > 0))
        def _():
            row = start + r
            for part_index in range(wide // LANES):
                block = pl.program_id(0) * (wide // LANES) + part_index
                lanes = slice(part_index * LANES, (part_index + 1) * LANES)
                ends = y_ref[block, 4 * both : POLE_OUT].astype(F32)
                part = [
                    y_ref[block, p * both + r * COLS : p * both + (r + 1) * COLS]
                    for p in range(4)
                ]
                pad[row + 1, 8 : 8 + COLS, lanes] = part[0].astype(F32)
                pad[row + 1, 7:8, lanes] = ends[2 * r : 2 * r + 1]
                pad[row + 1, 8 + COLS : 9 + COLS, lanes] = ends[2 * r + 1 : 2 * r + 2]
                dq_out[row, :, lanes] = part[1]
                dk_sum[row, :, lanes] += part[2].astype(F32)
                dv_sum[row, :, lanes] += part[3].astype(F32)

    dk_out[...] = dk_sum[...].astype(BF16)
    dv_out[...] = dv_sum[...].astype(BF16)
    mixed = pad[1 : 1 + ROWS, 8 : 8 + COLS]
    for a in range(3):
        for b in range(3):
            weight = conv_ref[3 * a + b : 3 * a + b + 1][None]
            mixed = mixed + weight * pad[a : a + ROWS, 7 + b : 7 + b + COLS]
    mixed_out[...] = mixed.astype(BF16)


def shift(array, axis, step, wrap):
    count = lax.axis_size(axis)
    route = [(i, (i + step) % count) for i in range(count) if wrap or 0 <= i + step < count]
    return lax.ppermute(array, axis, route)


def sds(shape, dtype=BF16):
    return jax.ShapeDtypeStruct(shape, dtype)


def cost(flops, moved):
    return pl.CostEstimate(flops=flops, bytes_accessed=moved, transcendentals=0)


def halo(*shape, wide):
    return pltpu.VMEM(shape + (wide,), F32)


def body(queries, keys, values, conv_kernel, cotangent, pattern, polar):
    width = queries.shape[2]
    lat_count = lax.axis_size("lat")
    tokens = ROWS * COLS
    pack = 512
    span = 256
    packed = functools.partial(lane_spec, wide=pack)
    spanned = functools.partial(lane_spec, wide=span)

    anywhere = pl.BlockSpec(memory_space=pl.ANY)

    east_pay, west_pay, pole_pay = pl.pallas_call(
        pack_lon_kernel,
        grid=(width // pack,),
        in_specs=[packed(ROWS, COLS)] * 4,
        out_specs=[packed(LON_TOK)] * 2
        + [pl.BlockSpec((pack // LANES, POLE_IN, LANES), lambda j: (j, 0, 0))],
        out_shape=[sds((LON_TOK, width))] * 2 + [sds((PAIRS, POLE_IN, LANES))],
        scratch_shapes=[halo(16, wide=pack)],
        compiler_params=params(GRANT),
        cost_estimate=cost(0, 3 * 2**20),
        name="pack_lon",
    )(queries, keys, values, cotangent)
    from_west = shift(east_pay, "lon", 1, True)
    from_east = shift(west_pay, "lon", -1, True)

    south_pay, north_pay = pl.pallas_call(
        pack_lat_kernel,
        grid=(width // pack,),
        in_specs=[packed(ROWS, COLS)] * 3 + [packed(LON_TOK)] * 2,
        out_specs=[packed(LAT_TOK)] * 2,
        out_shape=[sds((LAT_TOK, width))] * 2,
        scratch_shapes=[halo(16, wide=pack)],
        compiler_params=params(GRANT),
        cost_estimate=cost(0, 3 * 2**20),
        name="pack_lat",
    )(keys, values, cotangent, from_west, from_east)
    from_north = shift(south_pay, "lat", 1, False)
    from_south = shift(north_pay, "lat", -1, False)
    pole_pay, _ = lax.optimization_barrier((pole_pay, south_pay))
    pole_in = lax.all_to_all(pole_pay, "lon", 0, 0)

    att, dq_near, south_back, north_back, mid, kg = pl.pallas_call(
        window_kernel,
        grid=(width // span,),
        in_specs=[SMEM, SMEM]
        + [spanned(ROWS, COLS)] * 4
        + [spanned(LON_TOK)] * 2
        + [spanned(LAT_TOK)] * 2
        + [spanned(9)],
        out_specs=[
            spanned(tokens),
            spanned(tokens),
            spanned(BACK_LAT),
            spanned(BACK_LAT),
            spanned(2, 2 * tokens),
            spanned(9),
        ],
        out_shape=[
            sds((tokens, width)),
            sds((tokens, width)),
            sds((BACK_LAT, width)),
            sds((BACK_LAT, width)),
            sds((2, 2 * tokens, width), F32),
            sds((9, width), F32),
        ],
        scratch_shapes=[halo(ROWS + 2, 48, wide=span), pltpu.VMEM((4 * tokens, tokens), F32)],
        compiler_params=params(GRANT),
        cost_estimate=cost(4 * 10**9, 8 * 2**20),
        name="window",
    )(
        pattern.T, polar, queries, keys, values, cotangent, from_west, from_east,
        from_north, from_south, conv_kernel,
    )
    back_north = shift(south_back, "lat", 1, False)
    back_south = shift(north_back, "lat", -1, False)

    pole_out = pl.pallas_call(
        pole_kernel,
        in_specs=[SMEM] + [anywhere] * 3,
        out_specs=anywhere,
        out_shape=sds((PAIRS, POLE_OUT + 2 * KG_ROWS, LANES)),
        scratch_shapes=[
            pltpu.VMEM((PAIRS, POLE_IN, LANES), BF16),
            pltpu.VMEM((PAIRS, POLE_OUT, LANES), BF16),
            pltpu.VMEM((PAIRS, 16, LANES), F32),
            pltpu.VMEM((9, LANES), F32),
            pltpu.VMEM((9, width), F32),
            pltpu.VMEM((KG_ROWS, LANES), F32),
            pltpu.VMEM((2 * KG_ROWS, LANES), BF16),
            pltpu.SemaphoreType.DMA((PAIRS,)),
        ],
        compiler_params=params(GRANT, 0),
        cost_estimate=cost(10**9, 4 * 2**20),
        name="pole",
    )(polar, pole_in, conv_kernel, kg)
    pole_back = lax.all_to_all(pole_out, "lon", 0, 0)

    def summed(array, step):
        route = [(i, i ^ step) for i in range(lat_count)]
        return array + lax.ppermute(array, "lat", route)

    def after(array, *others):
        return lax.optimization_barrier((array,) + others)[0]

    west_back, east_back = pl.pallas_call(
        pack_back_kernel,
        grid=(width // pack,),
        in_specs=[
            pl.BlockSpec((2, tokens, pack), lambda j: (0, 1, j)),
            packed(tokens),
            packed(BACK_LAT),
            packed(BACK_LAT),
        ],
        out_specs=[packed(BACK_LON)] * 2,
        out_shape=[sds((BACK_LON, width))] * 2,
        scratch_shapes=[halo(16, wide=pack)],
        compiler_params=params(GRANT),
        cost_estimate=cost(0, 3 * 2**20),
        name="pack_back",
    )(mid, att, back_north, back_south)
    back_east = shift(west_back, "lon", -1, True)
    back_west = shift(east_back, "lon", 1, True)

    kg = jnp.sum(after(pole_back, west_back)[:, POLE_OUT:].astype(F32), axis=0)
    kg = kg[:KG_ROWS] + kg[KG_ROWS:]
    for step in (1, 2, 4):
        kg = summed(kg, step)
    kg, back_east, back_west = lax.optimization_barrier((kg, back_east, back_west))
    kg = summed(kg, 8)

    mixed, query_grad, key_grad, value_grad = pl.pallas_call(
        final_kernel,
        grid=(width // span,),
        in_specs=[
            SMEM,
            spanned(tokens),
            spanned(tokens),
            spanned(2, tokens),
            spanned(BACK_LAT),
            spanned(BACK_LAT),
            spanned(BACK_LON),
            spanned(BACK_LON),
        ]
        + [anywhere, spanned(9)],
        out_specs=[spanned(ROWS, COLS)] * 4,
        out_shape=[sds((ROWS, COLS, width))] * 4,
        scratch_shapes=[
            halo(ROWS + 2, 48, wide=span),
            halo(ROWS, COLS, wide=span),
            halo(ROWS, COLS, wide=span),
            pltpu.VMEM((PAIRS, POLE_OUT, LANES), BF16),
            pltpu.SemaphoreType.DMA((1,)),
        ],
        compiler_params=params(GRANT),
        cost_estimate=cost(0, 6 * 2**20),
        name="final",
    )(
        polar, att, dq_near, mid, back_north, back_south, back_west, back_east,
        pole_back, conv_kernel,
    )
    kg, mixed, query_grad, key_grad, value_grad = lax.optimization_barrier(
        (kg, mixed, query_grad, key_grad, value_grad)
    )
    kg = summed(kg, 16)[: 9 * PAIRS].reshape(PAIRS, 9, LANES) * (NLAT * NLON) ** (-0.5)
    kernel_grad = jnp.transpose(kg, (1, 0, 2)).reshape(9, width)
    return mixed, query_grad, key_grad, value_grad, kernel_grad


def solution(mesh):
    return jax.shard_map(
        body,
        mesh=mesh,
        in_specs=(
            P("lat", "lon", None),
            P("lat", "lon", None),
            P("lat", "lon", None),
            P(),
            P("lat", "lon", None),
            P(),
            P(),
        ),
        out_specs=(
            P("lat", "lon", None),
            P("lat", "lon", None),
            P("lat", "lon", None),
            P("lat", "lon", None),
            P(),
        ),
        check_vma=False,
    )
```

```python
import functools

import jax
import jax.numpy as jnp
from jax import lax
from jax.experimental import pallas as pl
from jax.experimental.pallas import tpu as pltpu
from jax.sharding import PartitionSpec as P

HEADS = 16
HEAD = 64
BLK = 8
REACH = 2
NLAT = 128
NLON = 256
ROWS = 4
COLS = 32
SIDE = REACH * BLK
LANES = 128
PAIRS = 8
NEG = -1e30
SCALE = HEAD ** (-0.5)
F32 = jnp.float32
BF16 = jnp.bfloat16
GRANT = 64

LON_TOK = 144
LAT_TOK = 160
CORNER_TOK = 144
BACK_LAT = 288
BACK_LON = 144
POLE_IN = 320
KG_ROWS = 80
POLE_OUT = 272


def params(mib, steps=1):
    return pltpu.CompilerParams(
        vmem_limit_bytes=mib * 2**20, dimension_semantics=("arbitrary",) * steps
    )


def lane_spec(*lead, wide=LANES):
    zeros = (0,) * len(lead)
    return pl.BlockSpec(lead + (wide,), lambda j: zeros + (j,))


SMEM = pl.BlockSpec(memory_space=pltpu.SMEM)


def nt(lhs, rhs):
    return lax.dot_general(lhs, rhs, (((1,), (1,)), ((), ())), preferred_element_type=F32)


def tn(lhs, rhs):
    return lax.dot_general(lhs, rhs, (((0,), (0,)), ((), ())), preferred_element_type=F32)


def nn(lhs, rhs):
    return lax.dot_general(lhs, rhs, (((1,), (0,)), ((), ())), preferred_element_type=F32)


def two_heads(array):
    first = lax.broadcasted_iota(jnp.int32, array.shape, 1) < HEAD
    return jnp.concatenate(
        [jnp.where(first, array, 0.0), jnp.where(first, 0.0, array)], axis=0
    ).astype(BF16)


def own_features(array):
    half = array.shape[1] // 2
    first = lax.broadcasted_iota(jnp.int32, (LANES, half), 0) < HEAD
    return jnp.where(first, array[:, :half], array[:, half:])


def attention(query, key, value, d_att, bias, valid):
    query2 = two_heads(query * SCALE)
    grad2 = two_heads(d_att)
    scores = nt(key, query2)
    if bias is not None:
        scores = scores + jnp.concatenate([bias, bias], axis=1)
    top = jnp.max(scores, axis=0, keepdims=True)
    weights = jnp.exp(scores - top)
    inverse = 1.0 / jnp.sum(weights, axis=0, keepdims=True)
    if valid is not None:
        inverse = inverse * jnp.concatenate([valid, valid], axis=1)
    att_t = own_features(tn(value, weights.astype(BF16)) * inverse).astype(BF16).astype(F32)
    product = d_att.T * att_t
    delta = jnp.concatenate(
        [
            jnp.sum(product[:HEAD], axis=0, keepdims=True),
            jnp.sum(product[HEAD:], axis=0, keepdims=True),
        ],
        axis=1,
    )
    probs = weights * inverse
    dscore = (probs * (nt(value, grad2) - delta)).astype(BF16)
    d_query = own_features(tn(key, dscore)).T * SCALE
    d_key = nn(dscore, query2)
    d_value = nn(probs.astype(BF16), grad2)
    return att_t.T, d_query, d_key, d_value


def place():
    lat = lax.axis_index("lat")
    return lat, lax.axis_index("lon"), jnp.where(lat == 0, 0, ROWS - REACH)


def at_pole(lat):
    return (lat == 0) | (lat == NLAT // ROWS - 1)


def run_copies(pairs, sems):
    copies = [
        pltpu.make_async_copy(source, target, sems.at[index])
        for index, (source, target) in enumerate(pairs)
    ]
    for copy in copies:
        copy.start()
    for copy in copies:
        copy.wait()


def pack_lon_kernel(q_ref, k_ref, v_ref, c_ref, east_ref, west_ref, south_ref, north_ref, pole_out, edge):
    half = ROWS * SIDE
    wide = edge.shape[1]
    for out, start, col in ((east_ref, COLS - SIDE, COLS - 1), (west_ref, 0, 0)):
        out[0:half] = k_ref[:, start : start + SIDE].reshape(half, wide)
        out[half : 2 * half] = v_ref[:, start : start + SIDE].reshape(half, wide)
        edge[...] = jnp.zeros_like(edge)
        for row in range(ROWS):
            cells = c_ref[row].astype(F32)
            edge[row : row + 1] = cells[col : col + 1]
        out[2 * half :] = edge[...].astype(BF16)
    lat, lon, start = place()
    both = REACH * COLS
    for out, first, row in ((south_ref, ROWS - REACH, ROWS - 1), (north_ref, 0, 0)):
        out[:both] = k_ref[first : first + REACH].reshape(both, wide)
        out[both : 2 * both] = v_ref[first : first + REACH].reshape(both, wide)
        out[2 * both :] = c_ref[row]

    @pl.when(at_pole(lat))
    def _():
        for part in range(wide // LANES):
            lanes = slice(part * LANES, (part + 1) * LANES)
            for index, ref in enumerate((q_ref, k_ref, v_ref)):
                pole_out[part, index * both : (index + 1) * both] = ref[
                    pl.ds(start, REACH), :, lanes
                ].reshape(both, LANES)
            pole_out[part, 3 * both :] = c_ref[:, :, lanes].reshape(ROWS * COLS, LANES)


def pack_corner_kernel(w_ref, e_ref, south_ref, north_ref, edge):
    side = REACH * SIDE
    half = ROWS * SIDE
    west_cot = w_ref[2 * half :].astype(F32)
    east_cot = e_ref[2 * half :].astype(F32)
    for out, start, row in ((south_ref, ROWS - REACH, ROWS - 1), (north_ref, 0, 0)):
        for index in range(2):
            near = index * half + start * SIDE
            out[2 * index * side : (2 * index + 1) * side] = w_ref[near : near + side]
            out[(2 * index + 1) * side : (2 * index + 2) * side] = e_ref[near : near + side]
        edge[...] = jnp.zeros_like(edge)
        edge[0:1] = west_cot[row : row + 1]
        edge[1:2] = east_cot[row : row + 1]
        out[4 * side :] = edge[...].astype(BF16)


def fill_rim(pad, row, middle, west, east):
    pad[row, 8 : 8 + COLS] = middle
    pad[row, 7:8] = west
    pad[row, 8 + COLS : 9 + COLS] = east


def key_groups():
    groups, start = [], 0
    for row_range in ((0, ROWS), (-REACH, REACH), (ROWS, REACH)):
        for first_col, width in ((0, COLS), (-SIDE, SIDE), (COLS, SIDE)):
            size = row_range[1] * width
            groups.append((start, size, row_range[0], width, first_col))
            start += size
    return groups


def window_kernel(
    pattern_ref, polar_ref, q_ref, k_ref, v_ref, c_ref, w_ref, e_ref,
    n_ref, s_ref, nc_ref, sc_ref, conv_ref,
    att_ref, dq_ref, south_ref, north_ref, mid_ref, kg_ref, pad, bias_ref,
):
    tokens = ROWS * COLS
    base = lax.axis_index("lat") * ROWS
    query_at = lax.broadcasted_iota(jnp.int32, (1, tokens), 1)
    query_row = query_at >> COLS.bit_length() - 1

    def by_row(values):
        out = jnp.full((1, tokens), values[0], values[0].dtype)
        for row in range(1, ROWS):
            out = jnp.where(query_row == row, values[row], out)
        return out

    valid = by_row([jnp.where(polar_ref[base + row] > 0, 0.0, 1.0) for row in range(ROWS)])

    @pl.when(pl.program_id(0) == 0)
    def _():
        offset = by_row([pattern_ref[0, base + row] for row in range(ROWS)])
        count = by_row([pattern_ref[1, base + row] for row in range(ROWS)])
        bits = BLK.bit_length() - 1
        block = ((query_at & COLS - 1) >> bits) + offset
        for start, size, first_row, width, first_col in key_groups():
            index = lax.broadcasted_iota(jnp.int32, (size, tokens), 0)
            row = (index >> width.bit_length() - 1) + first_row
            distance = ((index & width - 1) >> bits) + first_col // BLK - block
            inside = (jnp.abs(row - query_row) <= REACH) & (distance >= 0) & (distance < count)
            inside = inside & (base + row >= 0) & (base + row < NLAT)
            bias_ref[start : start + size] = jnp.where(inside, 0.0, NEG)

    half = ROWS * SIDE
    rim = 2 * REACH * SIDE + REACH * COLS
    wide = pad.shape[2]
    west_cot = w_ref[2 * half :].astype(F32)
    east_cot = e_ref[2 * half :].astype(F32)
    for row in range(ROWS):
        fill_rim(
            pad, row + 1, c_ref[row].astype(F32), west_cot[row : row + 1], east_cot[row : row + 1]
        )
    own = REACH * COLS
    corner = 2 * REACH * SIDE
    for row, ref, corner_ref in ((0, n_ref, nc_ref), (ROWS + 1, s_ref, sc_ref)):
        cells = corner_ref[2 * corner :].astype(F32)
        fill_rim(pad, row, ref[2 * own :].astype(F32), cells[0:1], cells[1:2])
    for part in range(wide // LANES):
        lanes = slice(part * LANES, (part + 1) * LANES)
        taps = [
            pad[2 - a : 2 - a + ROWS, 9 - b : 9 - b + COLS, lanes].reshape(tokens, LANES)
            for a in range(3)
            for b in range(3)
        ]
        back = taps[4]
        for tap in range(9):
            back = back + conv_ref[tap : tap + 1, lanes] * taps[tap]
        d_att = back.astype(BF16).astype(F32)
        key, value = (
            jnp.concatenate(
                [
                    ref[:, :, lanes].reshape(tokens, LANES),
                    w_ref[index * half : (index + 1) * half, lanes],
                    e_ref[index * half : (index + 1) * half, lanes],
                    n_ref[index * own : (index + 1) * own, lanes],
                    nc_ref[index * corner : (index + 1) * corner, lanes],
                    s_ref[index * own : (index + 1) * own, lanes],
                    sc_ref[index * corner : (index + 1) * corner, lanes],
                ],
                axis=0,
            )
            for index, ref in enumerate((k_ref, v_ref))
        )
        query = q_ref[:, :, lanes].reshape(tokens, LANES).astype(F32)
        att, d_query, d_key, d_value = attention(
            query, key, value, d_att, bias_ref[...], valid
        )
        att_b = att.astype(BF16)
        att_ref[:, lanes] = att_b
        dq_ref[:, lanes] = d_query.astype(BF16)
        near = tokens + 2 * half
        mid_ref[0, :, lanes] = d_key[:near]
        mid_ref[1, :, lanes] = d_value[:near]
        for ref, start, row in ((north_ref, near, 0), (south_ref, near + rim, ROWS - 1)):
            ref[:rim, lanes] = d_key[start : start + rim].astype(BF16)
            ref[rim : 2 * rim, lanes] = d_value[start : start + rim].astype(BF16)
            ref[2 * rim :, lanes] = att_b[row * COLS : (row + 1) * COLS]
        for tap in range(9):
            kg_ref[tap : tap + 1, lanes] = jnp.sum(att * taps[tap], axis=0, keepdims=True)


def pole_kernel(
    polar_ref, pole_in_ref, conv_ref, kgin_ref,
    out_ref, x_ref, y_ref, edge, weights_ref, kg_ref, kg_rows, kg_pair, sems,
):
    both = REACH * COLS
    lat, lon, start = place()
    base = lat * ROWS + start
    mine = pl.ds(pl.multiple_of(lon * LANES, LANES), LANES)
    run_copies([(kgin_ref, kg_ref)], sems)

    @pl.when(at_pole(lat))
    def _():
        run_copies([(conv_ref.at[:, mine], weights_ref), (pole_in_ref, x_ref)], sems)
        edge[...] = jnp.zeros_like(edge)
        weights = weights_ref[...]
        rows = []
        for step in range(REACH + 2):
            row = start + step - 1
            inside = jnp.where((row >= 0) & (row < ROWS), 1.0, 0.0)
            at = pl.multiple_of(3 * both + jnp.clip(row, 0, ROWS - 1) * COLS, COLS)
            rows.append(x_ref[:, pl.ds(at, COLS)].reshape(NLON, LANES).astype(F32) * inside)
        for r in range(REACH):
            taps = []
            back = rows[r + 1]
            for a in range(3):
                cells = rows[r + 2 - a]
                for b, shifted in enumerate(
                    (pltpu.roll(cells, NLON - 1, 0), cells, pltpu.roll(cells, 1, 0))
                ):
                    taps.append(shifted)
                    back = back + weights[3 * a + b : 3 * a + b + 1] * shifted
            query, key, value = (
                x_ref[:, part * both + r * COLS : part * both + (r + 1) * COLS].reshape(NLON, LANES)
                for part in range(3)
            )
            d_att = back.astype(BF16).astype(F32)
            att, d_query, d_key, d_value = attention(
                query.astype(F32), key, value, d_att, None, None
            )
            for part, array in enumerate((att, d_query, d_key, d_value)):
                y_ref[:, part * both + r * COLS : part * both + (r + 1) * COLS] = array.astype(
                    BF16
                ).reshape(PAIRS, COLS, LANES)
            for dest in range(PAIRS):
                west = (dest * COLS - 1) % NLON
                east = (dest * COLS + COLS) % NLON
                edge[dest, 2 * r : 2 * r + 1] = att[west : west + 1]
                edge[dest, 2 * r + 1 : 2 * r + 2] = att[east : east + 1]
            counted = jnp.where(polar_ref[base + r] > 0, 1.0, 0.0)
            for tap in range(9):
                kg_ref[tap : tap + 1, mine] += counted * jnp.sum(
                    att * taps[tap], axis=0, keepdims=True
                )
        y_ref[:, 4 * both :] = edge[...].astype(BF16)
        run_copies([(y_ref, out_ref.at[:, pl.ds(0, POLE_OUT)])], sems)

    kg_rows[...] = jnp.zeros_like(kg_rows)
    for block in range(PAIRS):
        kg_rows[9 * block : 9 * (block + 1)] = kg_ref[:, block * LANES : (block + 1) * LANES]
    high = kg_rows[...].astype(BF16)
    kg_pair[:KG_ROWS] = high
    kg_pair[KG_ROWS:] = (kg_rows[...] - high.astype(F32)).astype(BF16)
    tail = pl.ds(POLE_OUT, 2 * KG_ROWS)
    run_copies([(kg_pair, out_ref.at[dest, tail]) for dest in range(PAIRS)], sems)


def pack_back_kernel(mid_ref, att_ref, n_ref, s_ref, west_ref, east_ref, edge):
    half = ROWS * SIDE
    side = REACH * SIDE
    own = REACH * COLS
    rim = own + 2 * side
    for out, first, col in ((west_ref, 0, 0), (east_ref, 1, COLS - 1)):
        for index in range(2):
            source = index * rim + own + first * side
            cells = mid_ref[index, first * half : (first + 1) * half]
            out[index * half : index * half + side] = (
                cells[:side] + n_ref[source : source + side].astype(F32)
            ).astype(BF16)
            out[index * half + side : (index + 1) * half] = (
                cells[side:] + s_ref[source : source + side].astype(F32)
            ).astype(BF16)
        edge[...] = jnp.zeros_like(edge)
        edge[0:1] = n_ref[2 * rim :].astype(F32)[col : col + 1]
        edge[ROWS + 1 : ROWS + 2] = s_ref[2 * rim :].astype(F32)[col : col + 1]
        for row in range(ROWS):
            cells = att_ref[row * COLS : (row + 1) * COLS].astype(F32)
            edge[row + 1 : row + 2] = cells[col : col + 1]
        out[2 * half :] = edge[...].astype(BF16)


def final_kernel(
    polar_ref, att_ref, dq_ref, mid_ref, n_ref, s_ref, w_ref, e_ref,
    back_ref, conv_ref,
    mixed_out, dq_out, dk_out, dv_out, pad, dk_sum, dv_sum, y_ref, sems,
):
    half = ROWS * SIDE
    own = REACH * COLS
    both = own
    rim = own + 2 * REACH * SIDE
    west_att = w_ref[2 * half :].astype(F32)
    east_att = e_ref[2 * half :].astype(F32)
    middles = [n_ref[2 * rim :].astype(F32)]
    middles += [att_ref[row * COLS : (row + 1) * COLS].astype(F32) for row in range(ROWS)]
    middles += [s_ref[2 * rim :].astype(F32)]
    for row in range(ROWS + 2):
        fill_rim(pad, row, middles[row], west_att[row : row + 1], east_att[row : row + 1])
    dq_out[...] = dq_ref[...].reshape(ROWS, COLS, -1)
    wide = pad.shape[2]
    for index, total in ((0, dk_sum), (1, dv_sum)):
        north = n_ref[index * rim : index * rim + own].astype(F32)
        south = s_ref[index * rim : index * rim + own].astype(F32)
        cells = mid_ref[index] + jnp.concatenate([north, south], axis=0)
        sides = jnp.concatenate(
            [
                w_ref[index * half : (index + 1) * half].astype(F32).reshape(ROWS, SIDE, wide),
                e_ref[index * half : (index + 1) * half].astype(F32).reshape(ROWS, SIDE, wide),
            ],
            axis=1,
        )
        total[...] = cells.reshape(ROWS, COLS, wide) + sides
    lat, lon, start = place()

    @pl.when(at_pole(lat) & (pl.program_id(0) == 0))
    def _():
        run_copies([(back_ref.at[:, pl.ds(0, POLE_OUT)], y_ref)], sems)

    for r in range(REACH):

        @pl.when(at_pole(lat) & (polar_ref[lat * ROWS + start + r] > 0))
        def _():
            row = start + r
            for part_index in range(wide // LANES):
                block = pl.program_id(0) * (wide // LANES) + part_index
                lanes = slice(part_index * LANES, (part_index + 1) * LANES)
                ends = y_ref[block, 4 * both : POLE_OUT].astype(F32)
                part = [
                    y_ref[block, p * both + r * COLS : p * both + (r + 1) * COLS]
                    for p in range(4)
                ]
                pad[row + 1, 8 : 8 + COLS, lanes] = part[0].astype(F32)
                pad[row + 1, 7:8, lanes] = ends[2 * r : 2 * r + 1]
                pad[row + 1, 8 + COLS : 9 + COLS, lanes] = ends[2 * r + 1 : 2 * r + 2]
                dq_out[row, :, lanes] = part[1]
                dk_sum[row, :, lanes] += part[2].astype(F32)
                dv_sum[row, :, lanes] += part[3].astype(F32)

    dk_out[...] = dk_sum[...].astype(BF16)
    dv_out[...] = dv_sum[...].astype(BF16)
    mixed = pad[1 : 1 + ROWS, 8 : 8 + COLS]
    for a in range(3):
        for b in range(3):
            weight = conv_ref[3 * a + b : 3 * a + b + 1][None]
            mixed = mixed + weight * pad[a : a + ROWS, 7 + b : 7 + b + COLS]
    mixed_out[...] = mixed.astype(BF16)


def shift(array, axis, step, wrap):
    count = lax.axis_size(axis)
    route = [(i, (i + step) % count) for i in range(count) if wrap or 0 <= i + step < count]
    return lax.ppermute(array, axis, route)


def sds(shape, dtype=BF16):
    return jax.ShapeDtypeStruct(shape, dtype)


def cost(flops, moved):
    return pl.CostEstimate(flops=flops, bytes_accessed=moved, transcendentals=0)


def halo(*shape, wide):
    return pltpu.VMEM(shape + (wide,), F32)


def body(queries, keys, values, conv_kernel, cotangent, pattern, polar):
    width = queries.shape[2]
    lat_count = lax.axis_size("lat")
    tokens = ROWS * COLS
    pack = 512
    span = 256
    packed = functools.partial(lane_spec, wide=pack)
    spanned = functools.partial(lane_spec, wide=span)

    anywhere = pl.BlockSpec(memory_space=pl.ANY)

    east_pay, west_pay, south_pay, north_pay, pole_pay = pl.pallas_call(
        pack_lon_kernel,
        grid=(width // pack,),
        in_specs=[packed(ROWS, COLS)] * 4,
        out_specs=[packed(LON_TOK)] * 2
        + [packed(LAT_TOK)] * 2
        + [pl.BlockSpec((pack // LANES, POLE_IN, LANES), lambda j: (j, 0, 0))],
        out_shape=[sds((LON_TOK, width))] * 2
        + [sds((LAT_TOK, width))] * 2
        + [sds((PAIRS, POLE_IN, LANES))],
        scratch_shapes=[halo(16, wide=pack)],
        compiler_params=params(GRANT),
        cost_estimate=cost(0, 3 * 2**20),
        name="pack_lon",
    )(queries, keys, values, cotangent)
    from_west = shift(east_pay, "lon", 1, True)
    from_east = shift(west_pay, "lon", -1, True)

    from_north = shift(south_pay, "lat", 1, False)
    from_south = shift(north_pay, "lat", -1, False)
    south_corner, north_corner = pl.pallas_call(
        pack_corner_kernel,
        grid=(width // pack,),
        in_specs=[packed(LON_TOK)] * 2,
        out_specs=[packed(CORNER_TOK)] * 2,
        out_shape=[sds((CORNER_TOK, width))] * 2,
        scratch_shapes=[halo(16, wide=pack)],
        compiler_params=params(GRANT),
        cost_estimate=cost(0, 2 * 2**20),
        name="pack_corner",
    )(from_west, from_east)
    north_corners = shift(south_corner, "lat", 1, False)
    south_corners = shift(north_corner, "lat", -1, False)
    pole_pay, _ = lax.optimization_barrier((pole_pay, south_corner))
    pole_in = lax.all_to_all(pole_pay, "lon", 0, 0)

    att, dq_near, south_back, north_back, mid, kg = pl.pallas_call(
        window_kernel,
        grid=(width // span,),
        in_specs=[SMEM, SMEM]
        + [spanned(ROWS, COLS)] * 4
        + [spanned(LON_TOK)] * 2
        + [spanned(LAT_TOK)] * 2
        + [spanned(CORNER_TOK)] * 2
        + [spanned(9)],
        out_specs=[
            spanned(tokens),
            spanned(tokens),
            spanned(BACK_LAT),
            spanned(BACK_LAT),
            spanned(2, 2 * tokens),
            spanned(9),
        ],
        out_shape=[
            sds((tokens, width)),
            sds((tokens, width)),
            sds((BACK_LAT, width)),
            sds((BACK_LAT, width)),
            sds((2, 2 * tokens, width), F32),
            sds((9, width), F32),
        ],
        scratch_shapes=[halo(ROWS + 2, 48, wide=span), pltpu.VMEM((4 * tokens, tokens), F32)],
        compiler_params=params(GRANT),
        cost_estimate=cost(4 * 10**9, 8 * 2**20),
        name="window",
    )(
        pattern.T, polar, queries, keys, values, cotangent, from_west, from_east,
        from_north, from_south, north_corners, south_corners, conv_kernel,
    )
    back_north = shift(south_back, "lat", 1, False)
    back_south = shift(north_back, "lat", -1, False)

    pole_out = pl.pallas_call(
        pole_kernel,
        in_specs=[SMEM] + [anywhere] * 3,
        out_specs=anywhere,
        out_shape=sds((PAIRS, POLE_OUT + 2 * KG_ROWS, LANES)),
        scratch_shapes=[
            pltpu.VMEM((PAIRS, POLE_IN, LANES), BF16),
            pltpu.VMEM((PAIRS, POLE_OUT, LANES), BF16),
            pltpu.VMEM((PAIRS, 16, LANES), F32),
            pltpu.VMEM((9, LANES), F32),
            pltpu.VMEM((9, width), F32),
            pltpu.VMEM((KG_ROWS, LANES), F32),
            pltpu.VMEM((2 * KG_ROWS, LANES), BF16),
            pltpu.SemaphoreType.DMA((PAIRS,)),
        ],
        compiler_params=params(GRANT, 0),
        cost_estimate=cost(10**9, 4 * 2**20),
        name="pole",
    )(polar, pole_in, conv_kernel, kg)
    pole_back = lax.all_to_all(pole_out, "lon", 0, 0)

    def summed(array, step):
        route = [(i, i ^ step) for i in range(lat_count)]
        return array + lax.ppermute(array, "lat", route)

    def after(array, *others):
        return lax.optimization_barrier((array,) + others)[0]

    west_back, east_back = pl.pallas_call(
        pack_back_kernel,
        grid=(width // pack,),
        in_specs=[
            pl.BlockSpec((2, tokens, pack), lambda j: (0, 1, j)),
            packed(tokens),
            packed(BACK_LAT),
            packed(BACK_LAT),
        ],
        out_specs=[packed(BACK_LON)] * 2,
        out_shape=[sds((BACK_LON, width))] * 2,
        scratch_shapes=[halo(16, wide=pack)],
        compiler_params=params(GRANT),
        cost_estimate=cost(0, 3 * 2**20),
        name="pack_back",
    )(mid, att, back_north, back_south)
    back_east = shift(west_back, "lon", -1, True)
    back_west = shift(east_back, "lon", 1, True)

    kg = jnp.sum(after(pole_back, west_back)[:, POLE_OUT:].astype(F32), axis=0)
    kg = kg[:KG_ROWS] + kg[KG_ROWS:]
    for step in (1, 2, 4):
        kg = summed(kg, step)
    kg, back_east, back_west = lax.optimization_barrier((kg, back_east, back_west))
    kg = summed(kg, 8)

    mixed, query_grad, key_grad, value_grad = pl.pallas_call(
        final_kernel,
        grid=(width // span,),
        in_specs=[
            SMEM,
            spanned(tokens),
            spanned(tokens),
            spanned(2, tokens),
            spanned(BACK_LAT),
            spanned(BACK_LAT),
            spanned(BACK_LON),
            spanned(BACK_LON),
        ]
        + [anywhere, spanned(9)],
        out_specs=[spanned(ROWS, COLS)] * 4,
        out_shape=[sds((ROWS, COLS, width))] * 4,
        scratch_shapes=[
            halo(ROWS + 2, 48, wide=span),
            halo(ROWS, COLS, wide=span),
            halo(ROWS, COLS, wide=span),
            pltpu.VMEM((PAIRS, POLE_OUT, LANES), BF16),
            pltpu.SemaphoreType.DMA((1,)),
        ],
        compiler_params=params(GRANT),
        cost_estimate=cost(0, 6 * 2**20),
        name="final",
    )(
        polar, att, dq_near, mid, back_north, back_south, back_west, back_east,
        pole_back, conv_kernel,
    )
    kg, mixed, query_grad, key_grad, value_grad = lax.optimization_barrier(
        (kg, mixed, query_grad, key_grad, value_grad)
    )
    kg = summed(kg, 16)[: 9 * PAIRS].reshape(PAIRS, 9, LANES) * (NLAT * NLON) ** (-0.5)
    kernel_grad = jnp.transpose(kg, (1, 0, 2)).reshape(9, width)
    return mixed, query_grad, key_grad, value_grad, kernel_grad


def solution(mesh):
    return jax.shard_map(
        body,
        mesh=mesh,
        in_specs=(
            P("lat", "lon", None),
            P("lat", "lon", None),
            P("lat", "lon", None),
            P(),
            P("lat", "lon", None),
            P(),
            P(),
        ),
        out_specs=(
            P("lat", "lon", None),
            P("lat", "lon", None),
            P("lat", "lon", None),
            P("lat", "lon", None),
            P(),
        ),
        check_vma=False,
    )
```

```python
import functools

import jax
import jax.numpy as jnp
from jax import lax
from jax.experimental import pallas as pl
from jax.experimental.pallas import tpu as pltpu
from jax.sharding import PartitionSpec as P

HEADS = 16
HEAD = 64
BLK = 8
REACH = 2
NLAT = 128
NLON = 256
ROWS = 4
COLS = 32
SIDE = REACH * BLK
LANES = 128
PAIRS = 8
NEG = -1e30
SCALE = HEAD ** (-0.5)
F32 = jnp.float32
BF16 = jnp.bfloat16
GRANT = 64

LON_TOK = 144
LAT_TOK = 160
CORNER_TOK = 144
BACK_LAT = 288
BACK_LON = 144
POLE_IN = 320
KG_ROWS = 80
POLE_OUT = 272


def params(mib, steps=1):
    return pltpu.CompilerParams(
        vmem_limit_bytes=mib * 2**20, dimension_semantics=("arbitrary",) * steps
    )


def lane_spec(*lead, wide=LANES):
    zeros = (0,) * len(lead)
    return pl.BlockSpec(lead + (wide,), lambda j: zeros + (j,))


SMEM = pl.BlockSpec(memory_space=pltpu.SMEM)


def nt(lhs, rhs):
    return lax.dot_general(lhs, rhs, (((1,), (1,)), ((), ())), preferred_element_type=F32)


def tn(lhs, rhs):
    return lax.dot_general(lhs, rhs, (((0,), (0,)), ((), ())), preferred_element_type=F32)


def nn(lhs, rhs):
    return lax.dot_general(lhs, rhs, (((1,), (0,)), ((), ())), preferred_element_type=F32)


def two_heads(array):
    first = lax.broadcasted_iota(jnp.int32, array.shape, 1) < HEAD
    return jnp.concatenate(
        [jnp.where(first, array, 0.0), jnp.where(first, 0.0, array)], axis=0
    ).astype(BF16)


def own_features(array):
    half = array.shape[1] // 2
    first = lax.broadcasted_iota(jnp.int32, (LANES, half), 0) < HEAD
    return jnp.where(first, array[:, :half], array[:, half:])


def attention(query, key, value, d_att, bias, valid):
    query2 = two_heads(query * SCALE)
    grad2 = two_heads(d_att)
    scores = nt(key, query2)
    if bias is not None:
        scores = scores + jnp.concatenate([bias, bias], axis=1)
    top = jnp.max(scores, axis=0, keepdims=True)
    weights = jnp.exp(scores - top)
    inverse = 1.0 / jnp.sum(weights, axis=0, keepdims=True)
    if valid is not None:
        inverse = inverse * jnp.concatenate([valid, valid], axis=1)
    att_t = own_features(tn(value, weights.astype(BF16)) * inverse).astype(BF16).astype(F32)
    product = d_att.T * att_t
    delta = jnp.concatenate(
        [
            jnp.sum(product[:HEAD], axis=0, keepdims=True),
            jnp.sum(product[HEAD:], axis=0, keepdims=True),
        ],
        axis=1,
    )
    probs = weights * inverse
    dscore = (probs * (nt(value, grad2) - delta)).astype(BF16)
    d_query = own_features(tn(key, dscore)).T * SCALE
    d_key = nn(dscore, query2)
    d_value = nn(probs.astype(BF16), grad2)
    return att_t.T, d_query, d_key, d_value


def place():
    lat = lax.axis_index("lat")
    return lat, lax.axis_index("lon"), jnp.where(lat == 0, 0, ROWS - REACH)


def at_pole(lat):
    return (lat == 0) | (lat == NLAT // ROWS - 1)


def run_copies(pairs, sems):
    copies = [
        pltpu.make_async_copy(source, target, sems.at[index])
        for index, (source, target) in enumerate(pairs)
    ]
    for copy in copies:
        copy.start()
    for copy in copies:
        copy.wait()


def pack_lon_kernel(q_ref, k_ref, v_ref, c_ref, east_ref, west_ref, south_ref, north_ref, pole_out, edge):
    half = ROWS * SIDE
    wide = edge.shape[1]
    for out, start, col in ((east_ref, COLS - SIDE, COLS - 1), (west_ref, 0, 0)):
        out[0:half] = k_ref[:, start : start + SIDE].reshape(half, wide)
        out[half : 2 * half] = v_ref[:, start : start + SIDE].reshape(half, wide)
        edge[...] = jnp.zeros_like(edge)
        for row in range(ROWS):
            cells = c_ref[row].astype(F32)
            edge[row : row + 1] = cells[col : col + 1]
        out[2 * half :] = edge[...].astype(BF16)
    lat, lon, start = place()
    both = REACH * COLS
    for out, first, row in ((south_ref, ROWS - REACH, ROWS - 1), (north_ref, 0, 0)):
        out[:both] = k_ref[first : first + REACH].reshape(both, wide)
        out[both : 2 * both] = v_ref[first : first + REACH].reshape(both, wide)
        out[2 * both :] = c_ref[row]

    @pl.when(at_pole(lat))
    def _():
        for part in range(wide // LANES):
            lanes = slice(part * LANES, (part + 1) * LANES)
            for index, ref in enumerate((q_ref, k_ref, v_ref)):
                pole_out[part, index * both : (index + 1) * both] = ref[
                    pl.ds(start, REACH), :, lanes
                ].reshape(both, LANES)
            pole_out[part, 3 * both :] = c_ref[:, :, lanes].reshape(ROWS * COLS, LANES)


def pack_corner_kernel(w_ref, e_ref, south_ref, north_ref, edge):
    side = REACH * SIDE
    half = ROWS * SIDE
    west_cot = w_ref[2 * half :].astype(F32)
    east_cot = e_ref[2 * half :].astype(F32)
    for out, start, row in ((south_ref, ROWS - REACH, ROWS - 1), (north_ref, 0, 0)):
        for index in range(2):
            near = index * half + start * SIDE
            out[2 * index * side : (2 * index + 1) * side] = w_ref[near : near + side]
            out[(2 * index + 1) * side : (2 * index + 2) * side] = e_ref[near : near + side]
        edge[...] = jnp.zeros_like(edge)
        edge[0:1] = west_cot[row : row + 1]
        edge[1:2] = east_cot[row : row + 1]
        out[4 * side :] = edge[...].astype(BF16)


def fill_rim(pad, row, middle, west, east):
    pad[row, 8 : 8 + COLS] = middle
    pad[row, 7:8] = west
    pad[row, 8 + COLS : 9 + COLS] = east


def key_groups():
    groups, start = [], 0
    for row_range in ((0, ROWS), (-REACH, REACH), (ROWS, REACH)):
        for first_col, width in ((0, COLS), (-SIDE, SIDE), (COLS, SIDE)):
            size = row_range[1] * width
            groups.append((start, size, row_range[0], width, first_col))
            start += size
    return groups


def window_kernel(
    pattern_ref, polar_ref, q_ref, k_ref, v_ref, c_ref, w_ref, e_ref,
    n_ref, s_ref, nc_ref, sc_ref, conv_ref,
    att_ref, dq_ref, south_ref, north_ref, mid_ref, kg_ref, pad, bias_ref,
):
    tokens = ROWS * COLS
    base = lax.axis_index("lat") * ROWS
    query_at = lax.broadcasted_iota(jnp.int32, (1, tokens), 1)
    query_row = query_at >> COLS.bit_length() - 1

    def by_row(values):
        out = jnp.full((1, tokens), values[0], values[0].dtype)
        for row in range(1, ROWS):
            out = jnp.where(query_row == row, values[row], out)
        return out

    valid = by_row([jnp.where(polar_ref[base + row] > 0, 0.0, 1.0) for row in range(ROWS)])

    @pl.when(pl.program_id(0) == 0)
    def _():
        offset = by_row([pattern_ref[0, base + row] for row in range(ROWS)])
        count = by_row([pattern_ref[1, base + row] for row in range(ROWS)])
        bits = BLK.bit_length() - 1
        block = ((query_at & COLS - 1) >> bits) + offset
        for start, size, first_row, width, first_col in key_groups():
            index = lax.broadcasted_iota(jnp.int32, (size, tokens), 0)
            row = (index >> width.bit_length() - 1) + first_row
            distance = ((index & width - 1) >> bits) + first_col // BLK - block
            inside = (jnp.abs(row - query_row) <= REACH) & (distance >= 0) & (distance < count)
            inside = inside & (base + row >= 0) & (base + row < NLAT)
            bias_ref[start : start + size] = jnp.where(inside, 0.0, NEG)

    half = ROWS * SIDE
    rim = 2 * REACH * SIDE + REACH * COLS
    wide = pad.shape[2]
    west_cot = w_ref[2 * half :].astype(F32)
    east_cot = e_ref[2 * half :].astype(F32)
    for row in range(ROWS):
        fill_rim(
            pad, row + 1, c_ref[row].astype(F32), west_cot[row : row + 1], east_cot[row : row + 1]
        )
    own = REACH * COLS
    corner = 2 * REACH * SIDE
    for row, ref, corner_ref in ((0, n_ref, nc_ref), (ROWS + 1, s_ref, sc_ref)):
        cells = corner_ref[2 * corner :].astype(F32)
        fill_rim(pad, row, ref[2 * own :].astype(F32), cells[0:1], cells[1:2])
    for part in range(wide // LANES):
        lanes = slice(part * LANES, (part + 1) * LANES)
        taps = [
            pad[2 - a : 2 - a + ROWS, 9 - b : 9 - b + COLS, lanes].reshape(tokens, LANES)
            for a in range(3)
            for b in range(3)
        ]
        back = taps[4]
        for tap in range(9):
            back = back + conv_ref[tap : tap + 1, lanes] * taps[tap]
        d_att = back.astype(BF16).astype(F32)
        key, value = (
            jnp.concatenate(
                [
                    ref[:, :, lanes].reshape(tokens, LANES),
                    w_ref[index * half : (index + 1) * half, lanes],
                    e_ref[index * half : (index + 1) * half, lanes],
                    n_ref[index * own : (index + 1) * own, lanes],
                    nc_ref[index * corner : (index + 1) * corner, lanes],
                    s_ref[index * own : (index + 1) * own, lanes],
                    sc_ref[index * corner : (index + 1) * corner, lanes],
                ],
                axis=0,
            )
            for index, ref in enumerate((k_ref, v_ref))
        )
        query = q_ref[:, :, lanes].reshape(tokens, LANES).astype(F32)
        att, d_query, d_key, d_value = attention(
            query, key, value, d_att, bias_ref[...], valid
        )
        att_b = att.astype(BF16)
        att_ref[:, lanes] = att_b
        dq_ref[:, lanes] = d_query.astype(BF16)
        near = tokens + 2 * half
        mid_ref[0, :, lanes] = d_key[:near]
        mid_ref[1, :, lanes] = d_value[:near]
        for ref, start, row in ((north_ref, near, 0), (south_ref, near + rim, ROWS - 1)):
            ref[:rim, lanes] = d_key[start : start + rim].astype(BF16)
            ref[rim : 2 * rim, lanes] = d_value[start : start + rim].astype(BF16)
            ref[2 * rim :, lanes] = att_b[row * COLS : (row + 1) * COLS]
        for tap in range(9):
            kg_ref[tap : tap + 1, lanes] = jnp.sum(att * taps[tap], axis=0, keepdims=True)


def pole_kernel(
    polar_ref, pole_in_ref, conv_ref, kgin_ref,
    out_ref, x_ref, y_ref, edge, weights_ref, kg_ref, kg_rows, kg_pair, sems,
):
    both = REACH * COLS
    lat, lon, start = place()
    base = lat * ROWS + start
    mine = pl.ds(pl.multiple_of(lon * LANES, LANES), LANES)
    run_copies([(kgin_ref, kg_ref)], sems)

    @pl.when(at_pole(lat))
    def _():
        run_copies([(conv_ref.at[:, mine], weights_ref), (pole_in_ref, x_ref)], sems)
        edge[...] = jnp.zeros_like(edge)
        weights = weights_ref[...]
        rows = []
        for step in range(REACH + 2):
            row = start + step - 1
            inside = jnp.where((row >= 0) & (row < ROWS), 1.0, 0.0)
            at = pl.multiple_of(3 * both + jnp.clip(row, 0, ROWS - 1) * COLS, COLS)
            rows.append(x_ref[:, pl.ds(at, COLS)].reshape(NLON, LANES).astype(F32) * inside)
        for r in range(REACH):
            taps = []
            back = rows[r + 1]
            for a in range(3):
                cells = rows[r + 2 - a]
                for b, shifted in enumerate(
                    (pltpu.roll(cells, NLON - 1, 0), cells, pltpu.roll(cells, 1, 0))
                ):
                    taps.append(shifted)
                    back = back + weights[3 * a + b : 3 * a + b + 1] * shifted
            query, key, value = (
                x_ref[:, part * both + r * COLS : part * both + (r + 1) * COLS].reshape(NLON, LANES)
                for part in range(3)
            )
            d_att = back.astype(BF16).astype(F32)
            att, d_query, d_key, d_value = attention(
                query.astype(F32), key, value, d_att, None, None
            )
            for part, array in enumerate((att, d_query, d_key, d_value)):
                y_ref[:, part * both + r * COLS : part * both + (r + 1) * COLS] = array.astype(
                    BF16
                ).reshape(PAIRS, COLS, LANES)
            for dest in range(PAIRS):
                west = (dest * COLS - 1) % NLON
                east = (dest * COLS + COLS) % NLON
                edge[dest, 2 * r : 2 * r + 1] = att[west : west + 1]
                edge[dest, 2 * r + 1 : 2 * r + 2] = att[east : east + 1]
            counted = jnp.where(polar_ref[base + r] > 0, 1.0, 0.0)
            for tap in range(9):
                kg_ref[tap : tap + 1, mine] += counted * jnp.sum(
                    att * taps[tap], axis=0, keepdims=True
                )
        y_ref[:, 4 * both :] = edge[...].astype(BF16)
        run_copies([(y_ref, out_ref.at[:, pl.ds(0, POLE_OUT)])], sems)

    kg_rows[...] = jnp.zeros_like(kg_rows)
    for block in range(PAIRS):
        kg_rows[9 * block : 9 * (block + 1)] = kg_ref[:, block * LANES : (block + 1) * LANES]
    high = kg_rows[...].astype(BF16)
    kg_pair[:KG_ROWS] = high
    kg_pair[KG_ROWS:] = (kg_rows[...] - high.astype(F32)).astype(BF16)
    tail = pl.ds(POLE_OUT, 2 * KG_ROWS)
    run_copies([(kg_pair, out_ref.at[dest, tail]) for dest in range(PAIRS)], sems)


def pack_back_kernel(mid_ref, att_ref, n_ref, s_ref, west_ref, east_ref, edge):
    half = ROWS * SIDE
    side = REACH * SIDE
    own = REACH * COLS
    rim = own + 2 * side
    for out, first, col in ((west_ref, 0, 0), (east_ref, 1, COLS - 1)):
        for index in range(2):
            source = index * rim + own + first * side
            cells = mid_ref[index, first * half : (first + 1) * half]
            out[index * half : index * half + side] = (
                cells[:side] + n_ref[source : source + side].astype(F32)
            ).astype(BF16)
            out[index * half + side : (index + 1) * half] = (
                cells[side:] + s_ref[source : source + side].astype(F32)
            ).astype(BF16)
        edge[...] = jnp.zeros_like(edge)
        edge[0:1] = n_ref[2 * rim :].astype(F32)[col : col + 1]
        edge[ROWS + 1 : ROWS + 2] = s_ref[2 * rim :].astype(F32)[col : col + 1]
        for row in range(ROWS):
            cells = att_ref[row * COLS : (row + 1) * COLS].astype(F32)
            edge[row + 1 : row + 2] = cells[col : col + 1]
        out[2 * half :] = edge[...].astype(BF16)


def final_kernel(
    polar_ref, att_ref, dq_ref, mid_ref, n_ref, s_ref, w_ref, e_ref,
    back_ref, conv_ref,
    mixed_out, dq_out, dk_out, dv_out, pad, dk_sum, dv_sum, y_ref, sems,
):
    half = ROWS * SIDE
    own = REACH * COLS
    both = own
    rim = own + 2 * REACH * SIDE
    west_att = w_ref[2 * half :].astype(F32)
    east_att = e_ref[2 * half :].astype(F32)
    middles = [n_ref[2 * rim :].astype(F32)]
    middles += [att_ref[row * COLS : (row + 1) * COLS].astype(F32) for row in range(ROWS)]
    middles += [s_ref[2 * rim :].astype(F32)]
    for row in range(ROWS + 2):
        fill_rim(pad, row, middles[row], west_att[row : row + 1], east_att[row : row + 1])
    dq_out[...] = dq_ref[...].reshape(ROWS, COLS, -1)
    wide = pad.shape[2]
    for index, total in ((0, dk_sum), (1, dv_sum)):
        north = n_ref[index * rim : index * rim + own].astype(F32)
        south = s_ref[index * rim : index * rim + own].astype(F32)
        cells = mid_ref[index] + jnp.concatenate([north, south], axis=0)
        sides = jnp.concatenate(
            [
                w_ref[index * half : (index + 1) * half].astype(F32).reshape(ROWS, SIDE, wide),
                e_ref[index * half : (index + 1) * half].astype(F32).reshape(ROWS, SIDE, wide),
            ],
            axis=1,
        )
        total[...] = cells.reshape(ROWS, COLS, wide) + sides
    lat, lon, start = place()

    @pl.when(at_pole(lat) & (pl.program_id(0) == 0))
    def _():
        run_copies([(back_ref.at[:, pl.ds(0, POLE_OUT)], y_ref)], sems)

    for r in range(REACH):

        @pl.when(at_pole(lat) & (polar_ref[lat * ROWS + start + r] > 0))
        def _():
            row = start + r
            for part_index in range(wide // LANES):
                block = pl.program_id(0) * (wide // LANES) + part_index
                lanes = slice(part_index * LANES, (part_index + 1) * LANES)
                ends = y_ref[block, 4 * both : POLE_OUT].astype(F32)
                part = [
                    y_ref[block, p * both + r * COLS : p * both + (r + 1) * COLS]
                    for p in range(4)
                ]
                pad[row + 1, 8 : 8 + COLS, lanes] = part[0].astype(F32)
                pad[row + 1, 7:8, lanes] = ends[2 * r : 2 * r + 1]
                pad[row + 1, 8 + COLS : 9 + COLS, lanes] = ends[2 * r + 1 : 2 * r + 2]
                dq_out[row, :, lanes] = part[1]
                dk_sum[row, :, lanes] += part[2].astype(F32)
                dv_sum[row, :, lanes] += part[3].astype(F32)

    dk_out[...] = dk_sum[...].astype(BF16)
    dv_out[...] = dv_sum[...].astype(BF16)
    mixed = pad[1 : 1 + ROWS, 8 : 8 + COLS]
    for a in range(3):
        for b in range(3):
            weight = conv_ref[3 * a + b : 3 * a + b + 1][None]
            mixed = mixed + weight * pad[a : a + ROWS, 7 + b : 7 + b + COLS]
    mixed_out[...] = mixed.astype(BF16)


def shift(array, axis, step, wrap):
    count = lax.axis_size(axis)
    route = [(i, (i + step) % count) for i in range(count) if wrap or 0 <= i + step < count]
    return lax.ppermute(array, axis, route)


def sds(shape, dtype=BF16):
    return jax.ShapeDtypeStruct(shape, dtype)


def cost(flops, moved):
    return pl.CostEstimate(flops=flops, bytes_accessed=moved, transcendentals=0)


def halo(*shape, wide):
    return pltpu.VMEM(shape + (wide,), F32)


def body(queries, keys, values, conv_kernel, cotangent, pattern, polar):
    width = queries.shape[2]
    lat_count = lax.axis_size("lat")
    tokens = ROWS * COLS
    pack = 512
    span = 256
    packed = functools.partial(lane_spec, wide=pack)
    spanned = functools.partial(lane_spec, wide=span)

    anywhere = pl.BlockSpec(memory_space=pl.ANY)

    east_pay, west_pay, south_pay, north_pay, pole_pay = pl.pallas_call(
        pack_lon_kernel,
        grid=(width // pack,),
        in_specs=[packed(ROWS, COLS)] * 4,
        out_specs=[packed(LON_TOK)] * 2
        + [packed(LAT_TOK)] * 2
        + [pl.BlockSpec((pack // LANES, POLE_IN, LANES), lambda j: (j, 0, 0))],
        out_shape=[sds((LON_TOK, width))] * 2
        + [sds((LAT_TOK, width))] * 2
        + [sds((PAIRS, POLE_IN, LANES))],
        scratch_shapes=[halo(16, wide=pack)],
        compiler_params=params(GRANT),
        cost_estimate=cost(0, 3 * 2**20),
        name="pack_lon",
    )(queries, keys, values, cotangent)
    from_west = shift(east_pay, "lon", 1, True)
    from_east = shift(west_pay, "lon", -1, True)

    from_north = shift(south_pay, "lat", 1, False)
    from_south = shift(north_pay, "lat", -1, False)
    south_corner, north_corner = pl.pallas_call(
        pack_corner_kernel,
        grid=(width // pack,),
        in_specs=[packed(LON_TOK)] * 2,
        out_specs=[packed(CORNER_TOK)] * 2,
        out_shape=[sds((CORNER_TOK, width))] * 2,
        scratch_shapes=[halo(16, wide=pack)],
        compiler_params=params(GRANT),
        cost_estimate=cost(0, 2 * 2**20),
        name="pack_corner",
    )(from_west, from_east)
    north_corners = shift(south_corner, "lat", 1, False)
    south_corners = shift(north_corner, "lat", -1, False)
    pole_pay, _ = lax.optimization_barrier((pole_pay, south_corner))
    pole_in = lax.all_to_all(pole_pay, "lon", 0, 0)

    att, dq_near, south_back, north_back, mid, kg = pl.pallas_call(
        window_kernel,
        grid=(width // span,),
        in_specs=[SMEM, SMEM]
        + [spanned(ROWS, COLS)] * 4
        + [spanned(LON_TOK)] * 2
        + [spanned(LAT_TOK)] * 2
        + [spanned(CORNER_TOK)] * 2
        + [spanned(9)],
        out_specs=[
            spanned(tokens),
            spanned(tokens),
            spanned(BACK_LAT),
            spanned(BACK_LAT),
            spanned(2, 2 * tokens),
            spanned(9),
        ],
        out_shape=[
            sds((tokens, width)),
            sds((tokens, width)),
            sds((BACK_LAT, width)),
            sds((BACK_LAT, width)),
            sds((2, 2 * tokens, width), F32),
            sds((9, width), F32),
        ],
        scratch_shapes=[halo(ROWS + 2, 48, wide=span), pltpu.VMEM((4 * tokens, tokens), F32)],
        compiler_params=params(GRANT),
        cost_estimate=cost(4 * 10**9, 8 * 2**20),
        name="window",
    )(
        pattern.T, polar, queries, keys, values, cotangent, from_west, from_east,
        from_north, from_south, north_corners, south_corners, conv_kernel,
    )
    back_north = shift(south_back, "lat", 1, False)
    back_south = shift(north_back, "lat", -1, False)

    pole_out = pl.pallas_call(
        pole_kernel,
        in_specs=[SMEM] + [anywhere] * 3,
        out_specs=anywhere,
        out_shape=sds((PAIRS, POLE_OUT + 2 * KG_ROWS, LANES)),
        scratch_shapes=[
            pltpu.VMEM((PAIRS, POLE_IN, LANES), BF16),
            pltpu.VMEM((PAIRS, POLE_OUT, LANES), BF16),
            pltpu.VMEM((PAIRS, 16, LANES), F32),
            pltpu.VMEM((9, LANES), F32),
            pltpu.VMEM((9, width), F32),
            pltpu.VMEM((KG_ROWS, LANES), F32),
            pltpu.VMEM((2 * KG_ROWS, LANES), BF16),
            pltpu.SemaphoreType.DMA((PAIRS,)),
        ],
        compiler_params=params(GRANT, 0),
        cost_estimate=cost(10**9, 4 * 2**20),
        name="pole",
    )(polar, pole_in, conv_kernel, kg)
    pole_back = lax.all_to_all(pole_out, "lon", 0, 0)

    def summed(array, step):
        route = [(i, i ^ step) for i in range(lat_count)]
        return array + lax.ppermute(array, "lat", route)

    def after(array, *others):
        return lax.optimization_barrier((array,) + others)[0]

    west_back, east_back = pl.pallas_call(
        pack_back_kernel,
        grid=(width // pack,),
        in_specs=[
            pl.BlockSpec((2, tokens, pack), lambda j: (0, 1, j)),
            packed(tokens),
            packed(BACK_LAT),
            packed(BACK_LAT),
        ],
        out_specs=[packed(BACK_LON)] * 2,
        out_shape=[sds((BACK_LON, width))] * 2,
        scratch_shapes=[halo(16, wide=pack)],
        compiler_params=params(GRANT),
        cost_estimate=cost(0, 3 * 2**20),
        name="pack_back",
    )(mid, att, back_north, back_south)
    back_east = shift(west_back, "lon", -1, True)
    back_west = shift(east_back, "lon", 1, True)

    kg = jnp.sum(after(pole_back, west_back)[:, POLE_OUT:].astype(F32), axis=0)
    kg = kg[:KG_ROWS] + kg[KG_ROWS:]
    for step in (1, 4, 8):
        kg = summed(kg, step)
    kg, back_east, back_west = lax.optimization_barrier((kg, back_east, back_west))
    kg = summed(kg, 16)

    mixed, query_grad, key_grad, value_grad = pl.pallas_call(
        final_kernel,
        grid=(width // span,),
        in_specs=[
            SMEM,
            spanned(tokens),
            spanned(tokens),
            spanned(2, tokens),
            spanned(BACK_LAT),
            spanned(BACK_LAT),
            spanned(BACK_LON),
            spanned(BACK_LON),
        ]
        + [anywhere, spanned(9)],
        out_specs=[spanned(ROWS, COLS)] * 4,
        out_shape=[sds((ROWS, COLS, width))] * 4,
        scratch_shapes=[
            halo(ROWS + 2, 48, wide=span),
            halo(ROWS, COLS, wide=span),
            halo(ROWS, COLS, wide=span),
            pltpu.VMEM((PAIRS, POLE_OUT, LANES), BF16),
            pltpu.SemaphoreType.DMA((1,)),
        ],
        compiler_params=params(GRANT),
        cost_estimate=cost(0, 6 * 2**20),
        name="final",
    )(
        polar, att, dq_near, mid, back_north, back_south, back_west, back_east,
        pole_back, conv_kernel,
    )
    kg, mixed, query_grad, key_grad, value_grad = lax.optimization_barrier(
        (kg, mixed, query_grad, key_grad, value_grad)
    )
    kg = summed(kg, 2)[: 9 * PAIRS].reshape(PAIRS, 9, LANES) * (NLAT * NLON) ** (-0.5)
    kernel_grad = jnp.transpose(kg, (1, 0, 2)).reshape(9, width)
    return mixed, query_grad, key_grad, value_grad, kernel_grad


def solution(mesh):
    return jax.shard_map(
        body,
        mesh=mesh,
        in_specs=(
            P("lat", "lon", None),
            P("lat", "lon", None),
            P("lat", "lon", None),
            P(),
            P("lat", "lon", None),
            P(),
            P(),
        ),
        out_specs=(
            P("lat", "lon", None),
            P("lat", "lon", None),
            P("lat", "lon", None),
            P("lat", "lon", None),
            P(),
        ),
        check_vma=False,
    )
```

```python
import functools

import jax
import jax.numpy as jnp
from jax import lax
from jax.experimental import pallas as pl
from jax.experimental.pallas import tpu as pltpu
from jax.sharding import PartitionSpec as P

HEADS = 16
HEAD = 64
BLK = 8
REACH = 2
NLAT = 128
NLON = 256
ROWS = 4
COLS = 32
SIDE = REACH * BLK
LANES = 128
PAIRS = 8
NEG = -1e30
SCALE = HEAD ** (-0.5)
F32 = jnp.float32
BF16 = jnp.bfloat16
GRANT = 64

LON_TOK = 144
LAT_TOK = 160
CORNER_TOK = 144
BACK_LAT = 288
BACK_LON = 144
POLE_IN = 320
KG_ROWS = 80
POLE_OUT = 272


def params(mib, steps=1):
    return pltpu.CompilerParams(
        vmem_limit_bytes=mib * 2**20, dimension_semantics=("arbitrary",) * steps
    )


def lane_spec(*lead, wide=LANES):
    zeros = (0,) * len(lead)
    return pl.BlockSpec(lead + (wide,), lambda j: zeros + (j,))


SMEM = pl.BlockSpec(memory_space=pltpu.SMEM)


def nt(lhs, rhs):
    return lax.dot_general(lhs, rhs, (((1,), (1,)), ((), ())), preferred_element_type=F32)


def tn(lhs, rhs):
    return lax.dot_general(lhs, rhs, (((0,), (0,)), ((), ())), preferred_element_type=F32)


def nn(lhs, rhs):
    return lax.dot_general(lhs, rhs, (((1,), (0,)), ((), ())), preferred_element_type=F32)


def two_heads(array):
    first = lax.broadcasted_iota(jnp.int32, array.shape, 1) < HEAD
    return jnp.concatenate(
        [jnp.where(first, array, 0.0), jnp.where(first, 0.0, array)], axis=0
    ).astype(BF16)


def own_features(array):
    half = array.shape[1] // 2
    first = lax.broadcasted_iota(jnp.int32, (LANES, half), 0) < HEAD
    return jnp.where(first, array[:, :half], array[:, half:])


def attention(query, key, value, d_att, bias, valid):
    query2 = two_heads(query * SCALE)
    grad2 = two_heads(d_att)
    scores = nt(key, query2)
    if bias is not None:
        scores = scores + jnp.concatenate([bias, bias], axis=1)
    top = jnp.max(scores, axis=0, keepdims=True)
    weights = jnp.exp(scores - top)
    inverse = 1.0 / jnp.sum(weights, axis=0, keepdims=True)
    if valid is not None:
        inverse = inverse * jnp.concatenate([valid, valid], axis=1)
    att_t = own_features(tn(value, weights.astype(BF16)) * inverse).astype(BF16).astype(F32)
    product = d_att.T * att_t
    delta = jnp.concatenate(
        [
            jnp.sum(product[:HEAD], axis=0, keepdims=True),
            jnp.sum(product[HEAD:], axis=0, keepdims=True),
        ],
        axis=1,
    )
    probs = weights * inverse
    dscore = (probs * (nt(value, grad2) - delta)).astype(BF16)
    d_query = own_features(tn(key, dscore)).T * SCALE
    d_key = nn(dscore, query2)
    d_value = nn(probs.astype(BF16), grad2)
    return att_t.T, d_query, d_key, d_value


def place():
    lat = lax.axis_index("lat")
    return lat, lax.axis_index("lon"), jnp.where(lat == 0, 0, ROWS - REACH)


def at_pole(lat):
    return (lat == 0) | (lat == NLAT // ROWS - 1)


def run_copies(pairs, sems):
    copies = [
        pltpu.make_async_copy(source, target, sems.at[index])
        for index, (source, target) in enumerate(pairs)
    ]
    for copy in copies:
        copy.start()
    for copy in copies:
        copy.wait()


def pack_lon_kernel(q_ref, k_ref, v_ref, c_ref, east_ref, west_ref, south_ref, north_ref, pole_out, edge):
    half = ROWS * SIDE
    wide = edge.shape[1]
    for out, start, col in ((east_ref, COLS - SIDE, COLS - 1), (west_ref, 0, 0)):
        out[0:half] = k_ref[:, start : start + SIDE].reshape(half, wide)
        out[half : 2 * half] = v_ref[:, start : start + SIDE].reshape(half, wide)
        edge[...] = jnp.zeros_like(edge)
        for row in range(ROWS):
            cells = c_ref[row].astype(F32)
            edge[row : row + 1] = cells[col : col + 1]
        out[2 * half :] = edge[...].astype(BF16)
    lat, lon, start = place()
    both = REACH * COLS
    for out, first, row in ((south_ref, ROWS - REACH, ROWS - 1), (north_ref, 0, 0)):
        out[:both] = k_ref[first : first + REACH].reshape(both, wide)
        out[both : 2 * both] = v_ref[first : first + REACH].reshape(both, wide)
        out[2 * both :] = c_ref[row]

    @pl.when(at_pole(lat))
    def _():
        for part in range(wide // LANES):
            lanes = slice(part * LANES, (part + 1) * LANES)
            for index, ref in enumerate((q_ref, k_ref, v_ref)):
                pole_out[part, index * both : (index + 1) * both] = ref[
                    pl.ds(start, REACH), :, lanes
                ].reshape(both, LANES)
            pole_out[part, 3 * both :] = c_ref[:, :, lanes].reshape(ROWS * COLS, LANES)


def pack_corner_kernel(w_ref, e_ref, south_ref, north_ref, edge):
    side = REACH * SIDE
    half = ROWS * SIDE
    west_cot = w_ref[2 * half :].astype(F32)
    east_cot = e_ref[2 * half :].astype(F32)
    for out, start, row in ((south_ref, ROWS - REACH, ROWS - 1), (north_ref, 0, 0)):
        for index in range(2):
            near = index * half + start * SIDE
            out[2 * index * side : (2 * index + 1) * side] = w_ref[near : near + side]
            out[(2 * index + 1) * side : (2 * index + 2) * side] = e_ref[near : near + side]
        edge[...] = jnp.zeros_like(edge)
        edge[0:1] = west_cot[row : row + 1]
        edge[1:2] = east_cot[row : row + 1]
        out[4 * side :] = edge[...].astype(BF16)


def fill_rim(pad, row, middle, west, east):
    pad[row, 8 : 8 + COLS] = middle
    pad[row, 7:8] = west
    pad[row, 8 + COLS : 9 + COLS] = east


def key_groups():
    groups, start = [], 0
    for row_range in ((0, ROWS), (-REACH, REACH), (ROWS, REACH)):
        for first_col, width in ((0, COLS), (-SIDE, SIDE), (COLS, SIDE)):
            size = row_range[1] * width
            groups.append((start, size, row_range[0], width, first_col))
            start += size
    return groups


def window_kernel(
    pattern_ref, polar_ref, q_ref, k_ref, v_ref, c_ref, w_ref, e_ref,
    n_ref, s_ref, nc_ref, sc_ref, conv_ref,
    att_ref, dq_ref, south_ref, north_ref, mid_ref, kg_ref, pad, bias_ref,
):
    tokens = ROWS * COLS
    base = lax.axis_index("lat") * ROWS
    query_at = lax.broadcasted_iota(jnp.int32, (1, tokens), 1)
    query_row = query_at >> COLS.bit_length() - 1

    def by_row(values):
        out = jnp.full((1, tokens), values[0], values[0].dtype)
        for row in range(1, ROWS):
            out = jnp.where(query_row == row, values[row], out)
        return out

    valid = by_row([jnp.where(polar_ref[base + row] > 0, 0.0, 1.0) for row in range(ROWS)])

    @pl.when(pl.program_id(0) == 0)
    def _():
        offset = by_row([pattern_ref[0, base + row] for row in range(ROWS)])
        count = by_row([pattern_ref[1, base + row] for row in range(ROWS)])
        bits = BLK.bit_length() - 1
        block = ((query_at & COLS - 1) >> bits) + offset
        for start, size, first_row, width, first_col in key_groups():
            index = lax.broadcasted_iota(jnp.int32, (size, tokens), 0)
            row = (index >> width.bit_length() - 1) + first_row
            distance = ((index & width - 1) >> bits) + first_col // BLK - block
            inside = (jnp.abs(row - query_row) <= REACH) & (distance >= 0) & (distance < count)
            inside = inside & (base + row >= 0) & (base + row < NLAT)
            bias_ref[start : start + size] = jnp.where(inside, 0.0, NEG)

    half = ROWS * SIDE
    rim = 2 * REACH * SIDE + REACH * COLS
    wide = pad.shape[2]
    west_cot = w_ref[2 * half :].astype(F32)
    east_cot = e_ref[2 * half :].astype(F32)
    for row in range(ROWS):
        fill_rim(
            pad, row + 1, c_ref[row].astype(F32), west_cot[row : row + 1], east_cot[row : row + 1]
        )
    own = REACH * COLS
    corner = 2 * REACH * SIDE
    for row, ref, corner_ref in ((0, n_ref, nc_ref), (ROWS + 1, s_ref, sc_ref)):
        cells = corner_ref[2 * corner :].astype(F32)
        fill_rim(pad, row, ref[2 * own :].astype(F32), cells[0:1], cells[1:2])
    for part in range(wide // LANES):
        lanes = slice(part * LANES, (part + 1) * LANES)
        taps = [
            pad[2 - a : 2 - a + ROWS, 9 - b : 9 - b + COLS, lanes].reshape(tokens, LANES)
            for a in range(3)
            for b in range(3)
        ]
        back = taps[4]
        for tap in range(9):
            back = back + conv_ref[tap : tap + 1, lanes] * taps[tap]
        d_att = back.astype(BF16).astype(F32)
        key, value = (
            jnp.concatenate(
                [
                    ref[:, :, lanes].reshape(tokens, LANES),
                    w_ref[index * half : (index + 1) * half, lanes],
                    e_ref[index * half : (index + 1) * half, lanes],
                    n_ref[index * own : (index + 1) * own, lanes],
                    nc_ref[index * corner : (index + 1) * corner, lanes],
                    s_ref[index * own : (index + 1) * own, lanes],
                    sc_ref[index * corner : (index + 1) * corner, lanes],
                ],
                axis=0,
            )
            for index, ref in enumerate((k_ref, v_ref))
        )
        query = q_ref[:, :, lanes].reshape(tokens, LANES).astype(F32)
        att, d_query, d_key, d_value = attention(
            query, key, value, d_att, bias_ref[...], valid
        )
        att_b = att.astype(BF16)
        att_ref[:, lanes] = att_b
        dq_ref[:, lanes] = d_query.astype(BF16)
        near = tokens + 2 * half
        mid_ref[0, :, lanes] = d_key[:near]
        mid_ref[1, :, lanes] = d_value[:near]
        for ref, start, row in ((north_ref, near, 0), (south_ref, near + rim, ROWS - 1)):
            ref[:rim, lanes] = d_key[start : start + rim].astype(BF16)
            ref[rim : 2 * rim, lanes] = d_value[start : start + rim].astype(BF16)
            ref[2 * rim :, lanes] = att_b[row * COLS : (row + 1) * COLS]
        for tap in range(9):
            kg_ref[tap : tap + 1, lanes] = jnp.sum(att * taps[tap], axis=0, keepdims=True)


def pole_kernel(
    polar_ref, pole_in_ref, conv_ref, kgin_ref,
    out_ref, x_ref, y_ref, edge, weights_ref, kg_ref, kg_rows, kg_pair, sems,
):
    both = REACH * COLS
    lat, lon, start = place()
    base = lat * ROWS + start
    mine = pl.ds(pl.multiple_of(lon * LANES, LANES), LANES)
    run_copies([(kgin_ref, kg_ref)], sems)

    @pl.when(at_pole(lat))
    def _():
        run_copies([(conv_ref.at[:, mine], weights_ref), (pole_in_ref, x_ref)], sems)
        edge[...] = jnp.zeros_like(edge)
        weights = weights_ref[...]
        rows = []
        for step in range(REACH + 2):
            row = start + step - 1
            inside = jnp.where((row >= 0) & (row < ROWS), 1.0, 0.0)
            at = pl.multiple_of(3 * both + jnp.clip(row, 0, ROWS - 1) * COLS, COLS)
            rows.append(x_ref[:, pl.ds(at, COLS)].reshape(NLON, LANES).astype(F32) * inside)
        for r in range(REACH):
            taps = []
            back = rows[r + 1]
            for a in range(3):
                cells = rows[r + 2 - a]
                for b, shifted in enumerate(
                    (pltpu.roll(cells, NLON - 1, 0), cells, pltpu.roll(cells, 1, 0))
                ):
                    taps.append(shifted)
                    back = back + weights[3 * a + b : 3 * a + b + 1] * shifted
            query, key, value = (
                x_ref[:, part * both + r * COLS : part * both + (r + 1) * COLS].reshape(NLON, LANES)
                for part in range(3)
            )
            d_att = back.astype(BF16).astype(F32)
            att, d_query, d_key, d_value = attention(
                query.astype(F32), key, value, d_att, None, None
            )
            for part, array in enumerate((att, d_query, d_key, d_value)):
                y_ref[:, part * both + r * COLS : part * both + (r + 1) * COLS] = array.astype(
                    BF16
                ).reshape(PAIRS, COLS, LANES)
            for dest in range(PAIRS):
                west = (dest * COLS - 1) % NLON
                east = (dest * COLS + COLS) % NLON
                edge[dest, 2 * r : 2 * r + 1] = att[west : west + 1]
                edge[dest, 2 * r + 1 : 2 * r + 2] = att[east : east + 1]
            counted = jnp.where(polar_ref[base + r] > 0, 1.0, 0.0)
            for tap in range(9):
                kg_ref[tap : tap + 1, mine] += counted * jnp.sum(
                    att * taps[tap], axis=0, keepdims=True
                )
        y_ref[:, 4 * both :] = edge[...].astype(BF16)
        run_copies([(y_ref, out_ref.at[:, pl.ds(0, POLE_OUT)])], sems)

    kg_rows[...] = jnp.zeros_like(kg_rows)
    for block in range(PAIRS):
        kg_rows[9 * block : 9 * (block + 1)] = kg_ref[:, block * LANES : (block + 1) * LANES]
    high = kg_rows[...].astype(BF16)
    kg_pair[:KG_ROWS] = high
    kg_pair[KG_ROWS:] = (kg_rows[...] - high.astype(F32)).astype(BF16)
    tail = pl.ds(POLE_OUT, 2 * KG_ROWS)
    run_copies([(kg_pair, out_ref.at[dest, tail]) for dest in range(PAIRS)], sems)


def pack_back_kernel(mid_ref, att_ref, n_ref, s_ref, west_ref, east_ref, edge):
    half = ROWS * SIDE
    side = REACH * SIDE
    own = REACH * COLS
    rim = own + 2 * side
    for out, first, col in ((west_ref, 0, 0), (east_ref, 1, COLS - 1)):
        for index in range(2):
            source = index * rim + own + first * side
            cells = mid_ref[index, first * half : (first + 1) * half]
            out[index * half : index * half + side] = (
                cells[:side] + n_ref[source : source + side].astype(F32)
            ).astype(BF16)
            out[index * half + side : (index + 1) * half] = (
                cells[side:] + s_ref[source : source + side].astype(F32)
            ).astype(BF16)
        edge[...] = jnp.zeros_like(edge)
        edge[0:1] = n_ref[2 * rim :].astype(F32)[col : col + 1]
        edge[ROWS + 1 : ROWS + 2] = s_ref[2 * rim :].astype(F32)[col : col + 1]
        for row in range(ROWS):
            cells = att_ref[row * COLS : (row + 1) * COLS].astype(F32)
            edge[row + 1 : row + 2] = cells[col : col + 1]
        out[2 * half :] = edge[...].astype(BF16)


def final_kernel(
    polar_ref, att_ref, dq_ref, mid_ref, n_ref, s_ref, w_ref, e_ref,
    back_ref, conv_ref,
    mixed_out, dq_out, dk_out, dv_out, pad, dk_sum, dv_sum, y_ref, sems,
):
    half = ROWS * SIDE
    own = REACH * COLS
    both = own
    rim = own + 2 * REACH * SIDE
    west_att = w_ref[2 * half :].astype(F32)
    east_att = e_ref[2 * half :].astype(F32)
    middles = [n_ref[2 * rim :].astype(F32)]
    middles += [att_ref[row * COLS : (row + 1) * COLS].astype(F32) for row in range(ROWS)]
    middles += [s_ref[2 * rim :].astype(F32)]
    for row in range(ROWS + 2):
        fill_rim(pad, row, middles[row], west_att[row : row + 1], east_att[row : row + 1])
    dq_out[...] = dq_ref[...].reshape(ROWS, COLS, -1)
    wide = pad.shape[2]
    for index, total in ((0, dk_sum), (1, dv_sum)):
        north = n_ref[index * rim : index * rim + own].astype(F32)
        south = s_ref[index * rim : index * rim + own].astype(F32)
        cells = mid_ref[index] + jnp.concatenate([north, south], axis=0)
        sides = jnp.concatenate(
            [
                w_ref[index * half : (index + 1) * half].astype(F32).reshape(ROWS, SIDE, wide),
                e_ref[index * half : (index + 1) * half].astype(F32).reshape(ROWS, SIDE, wide),
            ],
            axis=1,
        )
        total[...] = cells.reshape(ROWS, COLS, wide) + sides
    lat, lon, start = place()

    @pl.when(at_pole(lat) & (pl.program_id(0) == 0))
    def _():
        run_copies([(back_ref.at[:, pl.ds(0, POLE_OUT)], y_ref)], sems)

    for r in range(REACH):

        @pl.when(at_pole(lat) & (polar_ref[lat * ROWS + start + r] > 0))
        def _():
            row = start + r
            for part_index in range(wide // LANES):
                block = pl.program_id(0) * (wide // LANES) + part_index
                lanes = slice(part_index * LANES, (part_index + 1) * LANES)
                ends = y_ref[block, 4 * both : POLE_OUT].astype(F32)
                part = [
                    y_ref[block, p * both + r * COLS : p * both + (r + 1) * COLS]
                    for p in range(4)
                ]
                pad[row + 1, 8 : 8 + COLS, lanes] = part[0].astype(F32)
                pad[row + 1, 7:8, lanes] = ends[2 * r : 2 * r + 1]
                pad[row + 1, 8 + COLS : 9 + COLS, lanes] = ends[2 * r + 1 : 2 * r + 2]
                dq_out[row, :, lanes] = part[1]
                dk_sum[row, :, lanes] += part[2].astype(F32)
                dv_sum[row, :, lanes] += part[3].astype(F32)

    dk_out[...] = dk_sum[...].astype(BF16)
    dv_out[...] = dv_sum[...].astype(BF16)
    mixed = pad[1 : 1 + ROWS, 8 : 8 + COLS]
    for a in range(3):
        for b in range(3):
            weight = conv_ref[3 * a + b : 3 * a + b + 1][None]
            mixed = mixed + weight * pad[a : a + ROWS, 7 + b : 7 + b + COLS]
    mixed_out[...] = mixed.astype(BF16)


def shift(array, axis, step, wrap):
    count = lax.axis_size(axis)
    route = [(i, (i + step) % count) for i in range(count) if wrap or 0 <= i + step < count]
    return lax.ppermute(array, axis, route)


def sds(shape, dtype=BF16):
    return jax.ShapeDtypeStruct(shape, dtype)


def cost(flops, moved):
    return pl.CostEstimate(flops=flops, bytes_accessed=moved, transcendentals=0)


def halo(*shape, wide):
    return pltpu.VMEM(shape + (wide,), F32)


def body(queries, keys, values, conv_kernel, cotangent, pattern, polar):
    width = queries.shape[2]
    lat_count = lax.axis_size("lat")
    tokens = ROWS * COLS
    pack = 512
    span = 512
    packed = functools.partial(lane_spec, wide=pack)
    spanned = functools.partial(lane_spec, wide=span)

    anywhere = pl.BlockSpec(memory_space=pl.ANY)

    east_pay, west_pay, south_pay, north_pay, pole_pay = pl.pallas_call(
        pack_lon_kernel,
        grid=(width // pack,),
        in_specs=[packed(ROWS, COLS)] * 4,
        out_specs=[packed(LON_TOK)] * 2
        + [packed(LAT_TOK)] * 2
        + [pl.BlockSpec((pack // LANES, POLE_IN, LANES), lambda j: (j, 0, 0))],
        out_shape=[sds((LON_TOK, width))] * 2
        + [sds((LAT_TOK, width))] * 2
        + [sds((PAIRS, POLE_IN, LANES))],
        scratch_shapes=[halo(16, wide=pack)],
        compiler_params=params(GRANT),
        cost_estimate=cost(0, 3 * 2**20),
        name="pack_lon",
    )(queries, keys, values, cotangent)
    from_west = shift(east_pay, "lon", 1, True)
    from_east = shift(west_pay, "lon", -1, True)

    from_north = shift(south_pay, "lat", 1, False)
    from_south = shift(north_pay, "lat", -1, False)
    south_corner, north_corner = pl.pallas_call(
        pack_corner_kernel,
        grid=(width // pack,),
        in_specs=[packed(LON_TOK)] * 2,
        out_specs=[packed(CORNER_TOK)] * 2,
        out_shape=[sds((CORNER_TOK, width))] * 2,
        scratch_shapes=[halo(16, wide=pack)],
        compiler_params=params(GRANT),
        cost_estimate=cost(0, 2 * 2**20),
        name="pack_corner",
    )(from_west, from_east)
    north_corners = shift(south_corner, "lat", 1, False)
    south_corners = shift(north_corner, "lat", -1, False)
    pole_pay, _ = lax.optimization_barrier((pole_pay, south_corner))
    pole_in = lax.all_to_all(pole_pay, "lon", 0, 0)

    att, dq_near, south_back, north_back, mid, kg = pl.pallas_call(
        window_kernel,
        grid=(width // span,),
        in_specs=[SMEM, SMEM]
        + [spanned(ROWS, COLS)] * 4
        + [spanned(LON_TOK)] * 2
        + [spanned(LAT_TOK)] * 2
        + [spanned(CORNER_TOK)] * 2
        + [spanned(9)],
        out_specs=[
            spanned(tokens),
            spanned(tokens),
            spanned(BACK_LAT),
            spanned(BACK_LAT),
            spanned(2, 2 * tokens),
            spanned(9),
        ],
        out_shape=[
            sds((tokens, width)),
            sds((tokens, width)),
            sds((BACK_LAT, width)),
            sds((BACK_LAT, width)),
            sds((2, 2 * tokens, width), F32),
            sds((9, width), F32),
        ],
        scratch_shapes=[halo(ROWS + 2, 48, wide=span), pltpu.VMEM((4 * tokens, tokens), F32)],
        compiler_params=params(GRANT),
        cost_estimate=cost(4 * 10**9, 8 * 2**20),
        name="window",
    )(
        pattern.T, polar, queries, keys, values, cotangent, from_west, from_east,
        from_north, from_south, north_corners, south_corners, conv_kernel,
    )
    back_north = shift(south_back, "lat", 1, False)
    back_south = shift(north_back, "lat", -1, False)

    pole_out = pl.pallas_call(
        pole_kernel,
        in_specs=[SMEM] + [anywhere] * 3,
        out_specs=anywhere,
        out_shape=sds((PAIRS, POLE_OUT + 2 * KG_ROWS, LANES)),
        scratch_shapes=[
            pltpu.VMEM((PAIRS, POLE_IN, LANES), BF16),
            pltpu.VMEM((PAIRS, POLE_OUT, LANES), BF16),
            pltpu.VMEM((PAIRS, 16, LANES), F32),
            pltpu.VMEM((9, LANES), F32),
            pltpu.VMEM((9, width), F32),
            pltpu.VMEM((KG_ROWS, LANES), F32),
            pltpu.VMEM((2 * KG_ROWS, LANES), BF16),
            pltpu.SemaphoreType.DMA((PAIRS,)),
        ],
        compiler_params=params(GRANT, 0),
        cost_estimate=cost(10**9, 4 * 2**20),
        name="pole",
    )(polar, pole_in, conv_kernel, kg)
    pole_back = lax.all_to_all(pole_out, "lon", 0, 0)

    def summed(array, step):
        route = [(i, i ^ step) for i in range(lat_count)]
        return array + lax.ppermute(array, "lat", route)

    def after(array, *others):
        return lax.optimization_barrier((array,) + others)[0]

    west_back, east_back = pl.pallas_call(
        pack_back_kernel,
        grid=(width // pack,),
        in_specs=[
            pl.BlockSpec((2, tokens, pack), lambda j: (0, 1, j)),
            packed(tokens),
            packed(BACK_LAT),
            packed(BACK_LAT),
        ],
        out_specs=[packed(BACK_LON)] * 2,
        out_shape=[sds((BACK_LON, width))] * 2,
        scratch_shapes=[halo(16, wide=pack)],
        compiler_params=params(GRANT),
        cost_estimate=cost(0, 3 * 2**20),
        name="pack_back",
    )(mid, att, back_north, back_south)
    back_east = shift(west_back, "lon", -1, True)
    back_west = shift(east_back, "lon", 1, True)

    kg = jnp.sum(after(pole_back, west_back)[:, POLE_OUT:].astype(F32), axis=0)
    kg = kg[:KG_ROWS] + kg[KG_ROWS:]
    for step in (1, 4, 8):
        kg = summed(kg, step)
    kg, back_east, back_west = lax.optimization_barrier((kg, back_east, back_west))
    kg = summed(kg, 16)

    mixed, query_grad, key_grad, value_grad = pl.pallas_call(
        final_kernel,
        grid=(width // span,),
        in_specs=[
            SMEM,
            spanned(tokens),
            spanned(tokens),
            spanned(2, tokens),
            spanned(BACK_LAT),
            spanned(BACK_LAT),
            spanned(BACK_LON),
            spanned(BACK_LON),
        ]
        + [anywhere, spanned(9)],
        out_specs=[spanned(ROWS, COLS)] * 4,
        out_shape=[sds((ROWS, COLS, width))] * 4,
        scratch_shapes=[
            halo(ROWS + 2, 48, wide=span),
            halo(ROWS, COLS, wide=span),
            halo(ROWS, COLS, wide=span),
            pltpu.VMEM((PAIRS, POLE_OUT, LANES), BF16),
            pltpu.SemaphoreType.DMA((1,)),
        ],
        compiler_params=params(GRANT),
        cost_estimate=cost(0, 6 * 2**20),
        name="final",
    )(
        polar, att, dq_near, mid, back_north, back_south, back_west, back_east,
        pole_back, conv_kernel,
    )
    kg, mixed, query_grad, key_grad, value_grad = lax.optimization_barrier(
        (kg, mixed, query_grad, key_grad, value_grad)
    )
    kg = summed(kg, 2)[: 9 * PAIRS].reshape(PAIRS, 9, LANES) * (NLAT * NLON) ** (-0.5)
    kernel_grad = jnp.transpose(kg, (1, 0, 2)).reshape(9, width)
    return mixed, query_grad, key_grad, value_grad, kernel_grad


def solution(mesh):
    return jax.shard_map(
        body,
        mesh=mesh,
        in_specs=(
            P("lat", "lon", None),
            P("lat", "lon", None),
            P("lat", "lon", None),
            P(),
            P("lat", "lon", None),
            P(),
            P(),
        ),
        out_specs=(
            P("lat", "lon", None),
            P("lat", "lon", None),
            P("lat", "lon", None),
            P("lat", "lon", None),
            P(),
        ),
        check_vma=False,
    )
```
